256 devices in a mesh: gx: 16 (over z_lo, x), gy: 4 (over y), gz: 4 (over z_hi, core).
Axes of the slice: x: 4, y: 4, z: 8 (z_hi: 2, z_lo: 4; z = z_hi * 4 + z_lo), core: 2. Of those that a mesh axis runs over, the one named last changes fastest.
Arguments:
- forcing: float32 [3, 256, 32, 512], P(None, 'gx', 'gy', 'gz'), may hold values from -6 to 6
- guess: float32 [3, 256, 32, 512], P(None, 'gx', 'gy', 'gz'), may hold values from -3 to 3
- lame_first: float32 [256, 32, 512], P('gx', 'gy', 'gz'), may hold values from 0.5 to 8
- shear_modulus: float32 [256, 32, 512], P('gx', 'gy', 'gz'), may hold values from 0.5 to 4
Outputs:
- solution: float32 [3, 256, 32, 512], P(None, 'gx', 'gy', 'gz')
- scaled_residual: float32 [3, 256, 32, 512], P(None, 'gx', 'gy', 'gz')
The draws below stay inside these ranges and needn't reach their ends.
All inputs are finite; a program needn't handle non-finite values.
Results may differ from the reference program's by a relative error of at most 0.0003.
Values sent between devices are 32-bit elements; how exact they have to be, the bound alone decides.
No kernel may reach another device: no remote copies, remote signals or barrier semaphores. Data moves between devices by JAX's collectives and lax.ppermute only.
A program may use at most 64 MiB of HBM per device.

```python
import math
import jax
import jax.numpy as jnp
import numpy as np
from jax import lax

CX = 16
NX = 256
NY = 32
NZ = 512
N_GX = 16


def levels(stream_key, dims, split, smallest, high):
    def one(position, shards_of):
        steps = jax.random.uniform(jax.random.fold_in(jax.random.fold_in(stream_key, 6), position), (shards_of,), jnp.float32, smallest / len(split), high / len(split))
        return jnp.repeat(jnp.exp(steps), dims[position] // shards_of).reshape((-1,) + (1,) * (len(dims) - position - 1))

    loudness = one(*split[0])
    for cut in split[1:]:
        loudness = loudness * one(*cut)
    return loudness


def centred(stream_key, extent, scale, most, shards=(), kind=jnp.bfloat16):
    loudness = levels(stream_key, extent, shards, -0.22, 0.18) if shards else 1.0
    array = jax.random.normal(stream_key, extent, jnp.float32) * scale * loudness
    return jnp.minimum(jnp.maximum(array, -most), most).astype(kind)


def setup_inputs(seed: int = 0) -> dict:
    arg_keys = jax.random.split(jax.random.key(seed), 5)
    return {
        "forcing": centred(arg_keys[0], (3, NX, NY, NZ), 1.0, 6.0, ((1, 16), (2, 4), (3, 4)), jnp.float32),
        "guess": centred(arg_keys[1], (3, NX, NY, NZ), 0.5, 3.0, ((1, 16), (2, 4), (3, 4)), jnp.float32),
        "lame_first": jnp.clip(jnp.exp(math.log(8.0) - 2.7725887 * jax.random.uniform(arg_keys[2], (NX, NY, NZ), jnp.float32) ** levels(arg_keys[2], (NX, NY, NZ), ((0, 16), (1, 4), (2, 4)), -0.2, 0.2)), 0.5, 8.0),
        "shear_modulus": jnp.clip(jnp.exp(math.log(4.0) - 2.0794415 * jax.random.uniform(arg_keys[3], (NX, NY, NZ), jnp.float32) ** levels(arg_keys[3], (NX, NY, NZ), ((0, 16), (1, 4), (2, 4)), -0.2, 0.2)), 0.5, 4.0),
    }


def element_tables():
    nodes_q = [(1.0 - 1.0 / math.sqrt(3.0)) / 2.0, (1.0 + 1.0 / math.sqrt(3.0)) / 2.0]
    k_lame = np.zeros((24, 24))
    k_shear = np.zeros((24, 24))
    for point_x in nodes_q:
        for point_y in nodes_q:
            for point_z in nodes_q:
                places = (point_x, point_y, point_z)
                grads = np.zeros((8, 3))
                for corner in range(8):
                    corner_bits = (corner >> 2 & 1, corner >> 1 & 1, corner & 1)
                    values = [places[d_idx] if corner_bits[d_idx] else 1.0 - places[d_idx] for d_idx in range(3)]
                    slopes = [1.0 if corner_bits[d_idx] else -1.0 for d_idx in range(3)]
                    grads[corner, 0] = slopes[0] * values[1] * values[2]
                    grads[corner, 1] = values[0] * slopes[1] * values[2]
                    grads[corner, 2] = values[0] * values[1] * slopes[2]
                for row_c in range(3):
                    for col_c in range(3):
                        block_l = 0.125 * np.outer(grads[:, row_c], grads[:, col_c])
                        block_s = 0.125 * np.outer(grads[:, col_c], grads[:, row_c])
                        if row_c == col_c:
                            block_s = block_s + 0.125 * grads @ grads.T
                        k_lame[row_c * 8:row_c * 8 + 8, col_c * 8:col_c * 8 + 8] += block_l
                        k_shear[row_c * 8:row_c * 8 + 8, col_c * 8:col_c * 8 + 8] += block_s
    return (k_lame, k_shear)

def element_forces(padded, lame_ext, shear_ext, stacked):
    ext_x, ext_y, ext_z = lame_ext.shape
    pieces = []
    for comp in range(3):
        for corner in range(8):
            bit_x, bit_y, bit_z = (corner >> 2 & 1, corner >> 1 & 1, corner & 1)
            pieces.append(padded[comp, bit_x:bit_x + ext_x, bit_y:bit_y + ext_y, bit_z:bit_z + ext_z])
    gathered = jnp.stack(pieces)
    products = jnp.einsum('rs,sxyz->rxyz', stacked, gathered, precision=lax.Precision.HIGHEST)
    forces = products[:24] * lame_ext + products[24:] * shear_ext
    size_x, size_y, size_z = (ext_x - 1, ext_y - 1, ext_z - 1)
    result = []
    for comp in range(3):
        total = jnp.zeros((size_x, size_y, size_z), jnp.float32)
        for corner in range(8):
            bit_x, bit_y, bit_z = (corner >> 2 & 1, corner >> 1 & 1, corner & 1)
            total = total + forces[comp * 8 + corner, 1 - bit_x:1 - bit_x + size_x, 1 - bit_y:1 - bit_y + size_y, 1 - bit_z:1 - bit_z + size_z]
        result.append(total)
    return jnp.stack(result)

def block_inverse(lame_ext, shear_ext, k_lame, k_shear):
    size_x, size_y, size_z = (lame_ext.shape[0] - 1, lame_ext.shape[1] - 1, lame_ext.shape[2] - 1)
    entries = [[jnp.zeros((size_x, size_y, size_z), jnp.float32) for col_c in range(3)] for row_c in range(3)]
    for corner in range(8):
        bit_x, bit_y, bit_z = (corner >> 2 & 1, corner >> 1 & 1, corner & 1)
        part_l = lame_ext[1 - bit_x:1 - bit_x + size_x, 1 - bit_y:1 - bit_y + size_y, 1 - bit_z:1 - bit_z + size_z]
        part_s = shear_ext[1 - bit_x:1 - bit_x + size_x, 1 - bit_y:1 - bit_y + size_y, 1 - bit_z:1 - bit_z + size_z]
        for row_c in range(3):
            for col_c in range(3):
                coef_l = float(k_lame[row_c * 8 + corner, col_c * 8 + corner])
                coef_s = float(k_shear[row_c * 8 + corner, col_c * 8 + corner])
                entries[row_c][col_c] = entries[row_c][col_c] + coef_l * part_l + coef_s * part_s
    e00, e01, e02 = entries[0]
    e10, e11, e12 = entries[1]
    e20, e21, e22 = entries[2]
    cof00 = e11 * e22 - e12 * e21
    cof01 = e12 * e20 - e10 * e22
    cof02 = e10 * e21 - e11 * e20
    determinant = e00 * cof00 + e01 * cof01 + e02 * cof02
    scale_inv = 1.0 / determinant
    inverse = [[cof00, e02 * e21 - e01 * e22, e01 * e12 - e02 * e11], [cof01, e00 * e22 - e02 * e20, e02 * e10 - e00 * e12], [cof02, e01 * e20 - e00 * e21, e00 * e11 - e01 * e10]]
    return [[inverse[row_c][col_c] * scale_inv for col_c in range(3)] for row_c in range(3)]

def apply_block(inverse, vector):
    return jnp.stack([inverse[row_c][0] * vector[0] + inverse[row_c][1] * vector[1] + inverse[row_c][2] * vector[2] for row_c in range(3)])

def reference(forcing, guess, lame_first, shear_modulus):
    k_lame, k_shear = element_tables()
    stacked = jnp.asarray(np.concatenate([k_lame, k_shear], 0), jnp.float32)
    lame_ext = jnp.pad(lame_first, ((1, 0), (1, 0), (1, 0)))
    shear_ext = jnp.pad(shear_modulus, ((1, 0), (1, 0), (1, 0)))
    inverse = block_inverse(lame_ext, shear_ext, k_lame, k_shear)

    def operator(field):
        padded = jnp.pad(field, ((0, 0), (1, 1), (1, 1), (1, 1)))

        def one_slab(index):
            start = (index * CX).astype(jnp.int32)
            slab_p = lax.dynamic_slice_in_dim(padded, start, CX + 2, 1)
            slab_l = lax.dynamic_slice_in_dim(lame_ext, start, CX + 1, 0)
            slab_s = lax.dynamic_slice_in_dim(shear_ext, start, CX + 1, 0)
            return element_forces(slab_p, slab_l, slab_s, stacked)
        slabs = lax.map(one_slab, jnp.arange(N_GX, dtype=jnp.int32))
        return jnp.moveaxis(slabs, 0, 1).reshape(3, NX, NY, NZ)
    low, high = (0.3, 3.0)
    theta = (high + low) / 2.0
    delta = (high - low) / 2.0
    sigma = theta / delta
    residual = forcing - operator(guess)
    step = apply_block(inverse, residual) / theta
    solution = guess + step
    rho_old = 1.0 / sigma
    for turn in range(2):
        residual = forcing - operator(solution)
        rho = 1.0 / (2.0 * sigma - rho_old)
        step = rho * rho_old * step + 2.0 * rho / delta * apply_block(inverse, residual)
        solution = solution + step
        rho_old = rho
    scaled_residual = apply_block(inverse, forcing - operator(solution))
    return (solution, scaled_residual)
```

```python
import itertools

import jax
import jax.numpy as jnp
from jax import lax
from jax.experimental import pallas as pl
from jax.experimental.pallas import tpu as pltpu
from jax.sharding import PartitionSpec as P

AXES = ("gx", "gy", "gz")
REACH = 4
F32 = jnp.float32
LANES = 128
ROWS = 8


def swap_pairs(dims, axis, kind):
    other = (1, 0, 1)[axis]

    def place(spot):
        return (spot[0] * dims[1] + spot[1]) * dims[2] + spot[2]

    pairs = []
    for spot in itertools.product(*(range(size) for size in dims)):
        goal = list(spot)
        mate = (spot[axis] ^ 1) if kind == 0 else ((spot[axis] + 1) ^ 1) - 1
        if 0 <= mate < dims[axis]:
            goal[axis] = mate
        else:
            goal[other] ^= 1
        pairs.append((place(spot), place(goal)))
    return pairs


def iota(shape, dim):
    return lax.broadcasted_iota(jnp.int32, shape, dim)


def half_turn(tile):
    return pltpu.roll(tile, ROWS // 2, 0)


def even(axis):
    return lax.rem(lax.axis_index(axis), 2) == 0


def at_end(axis):
    place = lax.axis_index(axis)
    return jnp.logical_or(place == 0, place == lax.axis_size(axis) - 1)


def fields_of(forcing, guess, lame, shear):
    return [guess.at[c] for c in range(3)] + [forcing.at[c] for c in range(3)] + [lame, shear]


def row_mask(flag):
    low = iota((ROWS, LANES), 0) < ROWS // 2
    return jnp.logical_xor(low, jnp.broadcast_to(flag, low.shape))


X_LAYERS = (4, 4, 4, 3, 3, 3, 4, 4, 4)
X_STARTS = tuple(sum(X_LAYERS[:f]) for f in range(9))
X_TILES = sum(X_LAYERS)


def pack_first(forcing, guess, lame, shear, own, z_near, z_far, y_near, y_far, x_near, x_far):
    fields = fields_of(forcing, guess, lame, shear)
    layers = own.shape[0]
    slot = lax.rem(iota((ROWS, LANES), 1), 16)
    group = lax.div(iota((ROWS, LANES), 1), 16)
    quarter = lax.div(slot, 4)
    edges = []
    for x in range(layers):
        low = jnp.zeros((ROWS, LANES), F32)
        high = low
        for f in range(8):
            tile = fields[f][x]
            low = jnp.where(group == f, pltpu.roll(tile, (16 * f + 4) % LANES, 1), low)
            high = jnp.where(group == f, pltpu.roll(tile, (16 * f + 12) % LANES, 1), high)
        tile = jnp.where(slot < 8, low, high)
        own[x] = tile
        edges.append(tile)
    up_first = even("gz")
    quads = layers // 4
    for q in range(quads):
        up = edges[q]
        down = edges[q]
        for j in range(4):
            tile = edges[q + quads * j]
            up = jnp.where(quarter == j, pltpu.roll(tile, (4 * j - 8) % LANES, 1), up)
            down = jnp.where(quarter == j, pltpu.roll(tile, (4 * j - 4) % LANES, 1), down)
        z_near[q] = jnp.where(up_first, up, down)
        z_far[q] = jnp.where(up_first, down, up)
    keep = row_mask(even("gy"))
    half = layers // 2
    for f in range(8):
        for x in range(half):
            here = fields[f][x]
            there = half_turn(fields[f][x + half])
            y_near[f * half + x] = jnp.where(keep, here, there)
            y_far[f * half + x] = jnp.where(keep, there, here)
    up_first = even("gx")
    for f in range(8):
        count = X_LAYERS[f]
        last = layers - count
        for x in range(count):
            x_near[X_STARTS[f] + x] = fields[f][jnp.where(up_first, last, 0) + x]
            x_far[X_STARTS[f] + x] = fields[f][jnp.where(up_first, 0, last) + x]


def pack_second(own, z_near, z_far, x_near_in, x_far_in, full, x_near, x_far):
    layers = own.shape[0]
    filled = pl.ds(0, X_STARTS[8])
    x_near[filled] = x_near_in[filled]
    x_far[filled] = x_far_in[filled]
    quads = layers // 4
    slot = lax.rem(iota((ROWS, LANES), 1), 16)
    forward = even("gz")
    ends = at_end("gz")
    for q in range(quads):
        near = z_near[q]
        far = jnp.where(ends, 0.0, z_far[q])
        behind = jnp.where(forward, far, near)
        ahead = jnp.where(forward, near, far)
        for j in range(4):
            x = q + quads * j
            tile = jnp.where(slot < 4, pltpu.roll(behind, (-4 * j) % LANES, 1), own[x])
            full[x] = jnp.where(slot >= 12, pltpu.roll(ahead, (12 - 4 * j) % LANES, 1), tile)
    up_first = even("gx")
    last = layers - 4
    for x in range(4):
        x_near[X_STARTS[8] + x] = full[jnp.where(up_first, last, 0) + x]
        x_far[X_STARTS[8] + x] = full[jnp.where(up_first, 0, last) + x]


def pack_third(full, x_near, x_far, y_near, y_far):
    keep = row_mask(even("gy"))
    half = full.shape[0] // 2
    for i in range(X_TILES):
        here = x_near[i]
        there = half_turn(x_far[i])
        y_near[i] = jnp.where(keep, here, there)
        y_far[i] = jnp.where(keep, there, here)
    for x in range(half):
        here = full[x]
        there = half_turn(full[x + half])
        y_near[X_TILES + x] = jnp.where(keep, here, there)
        y_far[X_TILES + x] = jnp.where(keep, there, here)


def row_next(tile):
    return pltpu.roll(tile, tile.shape[0] - 1, 0)


def row_prev(tile):
    return pltpu.roll(tile, 1, 0)


def lane_next(tile):
    return pltpu.roll(tile, LANES - 1, 1)


def lane_prev(tile):
    return pltpu.roll(tile, 1, 1)


def node_modes(here, beyond):
    total = here + beyond
    change = beyond - here
    total_y = row_next(total)
    change_y = row_next(change)
    return (total + total_y, total_y - total, change + change_y, change_y - change)


def element_modes(lower, upper, lam, mu):
    s = [[lower[c][m] + upper[c][m] for m in range(4)] for c in range(3)]
    d = [[upper[c][m] - lower[c][m] for m in range(4)] for c in range(3)]
    mu2 = mu + mu
    lam3 = lam * (1.0 / 3.0)
    mu3 = mu * (1.0 / 3.0)
    stiff = (lam3 + 4.0 * mu3) * (1.0 / 3.0)
    pressure = lam * (d[0][0] + s[1][1] + s[2][2])
    xx = pressure + mu2 * d[0][0]
    yy = pressure + mu2 * s[1][1]
    zz = pressure + mu2 * s[2][2]
    xy = mu * (s[0][1] + d[1][0])
    xz = mu * (s[0][2] + d[2][0])
    yz = mu * (s[1][2] + s[2][1])
    along_y = lam3 * (d[0][1] + s[2][3])
    along_z = lam3 * (d[0][2] + s[1][3])
    along_x = lam3 * (d[1][1] + d[2][2])
    twist = mu3 * (s[0][3] + d[1][2] + d[2][1])
    fs = [
        [None, xy, xz, twist + mu3 * s[0][3]],
        [None, yy, yz, along_z + mu * s[1][3]],
        [None, yz, zz, along_y + mu * s[2][3]],
    ]
    fd = [
        [xx, along_y + mu * d[0][1], along_z + mu * d[0][2], stiff * d[0][3]],
        [xy, along_x + mu * d[1][1], twist + mu3 * d[1][2], stiff * d[1][3]],
        [xz, twist + mu3 * d[2][1], along_x + mu * d[2][2], stiff * d[2][3]],
    ]
    low = [[-fd[c][0]] + [fs[c][m] - fd[c][m] for m in range(1, 4)] for c in range(3)]
    high = [[fd[c][0]] + [fs[c][m] + fd[c][m] for m in range(1, 4)] for c in range(3)]
    return low, high


def gather_rows(modes):
    total = (modes[0] - modes[1]) + row_prev(modes[0] + modes[1])
    change = (modes[2] - modes[3]) + row_prev(modes[2] + modes[3])
    return total - change, total + change


def apply_inverse(inv, vec):
    return (
        inv[0] * vec[0] + inv[1] * vec[1] + inv[2] * vec[2],
        inv[1] * vec[0] + inv[3] * vec[1] + inv[4] * vec[2],
        inv[2] * vec[0] + inv[4] * vec[1] + inv[5] * vec[2],
    )


def block_parts(lam, mu, shift):
    stiff = lam + 4.0 * mu
    cross = lam + mu
    stiff = stiff + shift[0](stiff)
    behind = shift[1](cross)
    total = behind + cross
    change = behind - cross
    total_y = row_prev(total)
    change_y = row_prev(change)
    return (stiff + row_prev(stiff), total_y - total, change_y + change, change_y - change)


def block_inverse(before, after, valid):
    diag = (16.0 / 9.0) * (before[0] + after[0])
    p = (4.0 / 3.0) * (before[1] - after[1])
    q = (4.0 / 3.0) * (before[2] - after[2])
    s = (4.0 / 3.0) * (before[3] + after[3])
    c00 = diag * diag - s * s
    c01 = q * s - p * diag
    c02 = p * s - q * diag
    scale = 1.0 / (diag * c00 + p * c01 + q * c02)
    cof = (c00, c01, c02, diag * diag - q * q, p * q - diag * s, diag * diag - p * p)
    return [jnp.where(valid, entry * scale, 0.0) for entry in cof]


def step_weights():
    low, high = (0.3, 3.0)
    theta = (high + low) / 2.0
    delta = (high - low) / 2.0
    sigma = theta / delta
    weights = [(0.0, 1.0 / theta)]
    rho_old = 1.0 / sigma
    for _ in range(2):
        rho = 1.0 / (2.0 * sigma - rho_old)
        weights.append((rho * rho_old, 2.0 * rho / delta))
        rho_old = rho
    return weights


def smooth(
    forcing, guess, lame, shear, full, y0_near, y0_far, x_near, x_far, y1_near, y1_far,
    out_solution, out_residual,
    field, edge, strip, strip_inv, strip_step, strip_push, inv, step, modes, forces,
):
    own_fields = fields_of(forcing, guess, lame, shear)
    layers = full.shape[0]
    wide = layers + 2 * REACH
    half = layers // 2
    tall = 2 * ROWS

    y_keep = row_mask(jnp.logical_not(even("gy")))
    y_ends = at_end("gy")
    x_forward = even("gx")
    x_ends = at_end("gx")

    def scaled(f, tile):
        return tile * (1.0 / 16.0) if f in (6, 7) else tile

    def beside(near, far):
        far = jnp.where(y_ends, 0.0, far)
        return jnp.where(y_keep, near, far), half_turn(jnp.where(y_keep, far, near))

    def target(f):
        return field.at[f] if f < 8 else edge

    zero = jnp.zeros((tall, LANES), F32)
    for f in range(3, 6):
        field[f, 0] = zero
        field[f, wide - 1] = zero
    for f in range(9):
        for x in range(half):
            if f < 8:
                i = f * half + x
                first, second = beside(y0_near[i], y0_far[i])
                target(f)[REACH + x, :ROWS] = scaled(f, own_fields[f][x])
                target(f)[REACH + x + half, :ROWS] = scaled(f, own_fields[f][x + half])
            else:
                i = X_TILES + x
                first, second = beside(y1_near[i], y1_far[i])
                edge[REACH + x, :ROWS] = full[x]
                edge[REACH + x + half, :ROWS] = full[x + half]
            target(f)[REACH + x, ROWS:] = scaled(f, first)
            target(f)[REACH + x + half, ROWS:] = scaled(f, second)
    for f in range(9):
        count = X_LAYERS[f]
        ahead = REACH + layers
        behind = REACH - count
        to_near = jnp.where(x_forward, ahead, behind)
        to_far = jnp.where(x_forward, behind, ahead)
        for x in range(count):
            i = X_STARTS[f] + x
            target(f)[to_near + x, :ROWS] = scaled(f, x_near[i])
            target(f)[to_far + x, :ROWS] = jnp.where(x_ends, 0.0, scaled(f, x_far[i]))
            first, second = beside(y1_near[i], y1_far[i])
            target(f)[to_near + x, ROWS:] = scaled(f, first)
            target(f)[to_far + x, ROWS:] = jnp.where(x_ends, 0.0, scaled(f, second))

    lane = iota((tall, LANES), 1)
    row = iota((tall, LANES), 0)
    group = lax.div(lane, 16)
    slot = lax.rem(lane, 16)
    first_lane = lane == 0
    last_lane = lane == LANES - 1

    groups = wide // 3
    for i in range(3):
        for f in range(8):
            tile = zero
            for g in range(groups):
                moved = pltpu.roll(edge[3 * g + i], (16 * (g - f)) % LANES, 1)
                tile = jnp.where(group == g, moved, tile)
            strip[f, i] = scaled(f, tile)

    place_x, place_y, place_z = (lax.axis_index(axis) for axis in AXES)
    count_x, count_y, count_z = (lax.axis_size(axis) for axis in AXES)
    from_x = jnp.where(place_x == 0, REACH, 0)
    to_x = jnp.where(place_x == count_x - 1, REACH + layers, wide)
    row_from = jnp.where(place_y == count_y - 1, ROWS + 4, ROWS)
    row_to = jnp.where(place_y == 0, ROWS + 4, tall)
    row_ok = jnp.logical_or(row < ROWS, jnp.logical_and(row >= row_from, row < row_to))
    slot_from = jnp.where(place_z == 0, 4, 0)
    slot_to = jnp.where(place_z == count_z - 1, 12, 16)
    slot_ok = jnp.logical_and(row_ok, jnp.logical_and(slot >= slot_from, slot < slot_to))

    def strip_next(tiles):
        return [tiles[1], tiles[2], pltpu.roll(tiles[0], LANES - 16, 1)]

    def strip_prev(tiles):
        return [pltpu.roll(tiles[2], 16, 1), tiles[0], tiles[1]]

    def at_high(tile, g):
        return pltpu.roll(tile, lax.rem(LANES + 115 - 16 * g, LANES), 1)

    def at_low(tile, g):
        return pltpu.roll(tile, lax.rem(LANES + 125 - 16 * g, LANES), 1)

    parts = [block_parts(strip[6, i], strip[7, i], (lane_prev, lane_prev)) for i in range(3)]
    previous = [strip_prev([parts[i][k] for i in range(3)]) for k in range(4)]
    for i in range(3):
        layer = 3 * group + i
        valid = jnp.logical_and(slot_ok, jnp.logical_and(layer >= from_x, layer < to_x))
        entries = block_inverse([previous[k][i] for k in range(4)], parts[i], valid)
        for k in range(6):
            strip_inv[k, i] = entries[k]

    def main_parts(x):
        g = lax.div(x, 3)
        i = lax.rem(x, 3)
        lam_low = at_low(strip[6, i], g)
        mu_low = at_low(strip[7, i], g)

        def shift_stiff(tile):
            return jnp.where(first_lane, lam_low + 4.0 * mu_low, lane_prev(tile))

        def shift_cross(tile):
            return jnp.where(first_lane, lam_low + mu_low, lane_prev(tile))

        return block_parts(field[6, x], field[7, x], (shift_stiff, shift_cross))

    def inverse_body(x, before):
        after = main_parts(x)
        valid = jnp.logical_and(row_ok, jnp.logical_and(x >= from_x, x < to_x))
        entries = block_inverse(before, after, valid)
        for k in range(6):
            inv[k, x] = entries[k]
        return after

    lax.fori_loop(1, wide - 1, inverse_body, main_parts(0))

    weights = step_weights()
    for turn in range(4):
        final = turn == 3
        here = [[strip[c, i] for i in range(3)] for c in range(3)]
        node = [[node_modes(here[c][i], lane_next(here[c][i])) for c in range(3)] for i in range(3)]
        above = [[[None] * 4 for c in range(3)] for i in range(3)]
        for c in range(3):
            for m in range(4):
                moved = strip_next([node[i][c][m] for i in range(3)])
                for i in range(3):
                    above[i][c][m] = moved[i]
        push = [element_modes(node[i], above[i], strip[6, i], strip[7, i]) for i in range(3)]
        pull = [[None] * 3 for i in range(3)]
        for c in range(3):
            total = [[None] * 4 for i in range(3)]
            for m in range(4):
                moved = strip_prev([push[i][1][c][m] for i in range(3)])
                for i in range(3):
                    total[i][m] = moved[i] + push[i][0][c][m]
            for i in range(3):
                stay, go = gather_rows(total[i])
                strip_push[c, i] = go
                pull[i][c] = stay + lane_prev(go)

        low, high = 1 + turn, wide - 1 - turn

        def modes_body(x, carry):
            g = lax.div(x, 3)
            i = lax.rem(x, 3)
            for c in range(3):
                tile = field[c, x]
                beyond = jnp.where(last_lane, at_high(strip[c, i], g), lane_next(tile))
                for m, value in enumerate(node_modes(tile, beyond)):
                    modes[x, 4 * c + m] = value
            return carry

        lax.fori_loop(low - 1, high + 1, modes_body, 0)

        if not final:
            keep, add = weights[turn]
            for i in range(3):
                rest = [strip[3 + c, i] - pull[i][c] for c in range(3)]
                moved = apply_inverse([strip_inv[k, i] for k in range(6)], rest)
                for c in range(3):
                    change = add * moved[c]
                    if turn > 0:
                        change = keep * strip_step[c, i] + change
                    strip_step[c, i] = change
                    strip[c, i] = strip[c, i] + change

        for part in range(2):
            rows = pl.ds(part * ROWS, ROWS)

            def load_modes(x, rows=rows):
                return [[modes[x, 4 * c + m, rows] for m in range(4)] for c in range(3)]

            def forces_body(x, carry, rows=rows, load_modes=load_modes):
                lower, pushed = carry
                upper = load_modes(x + 1)
                down, up = element_modes(lower, upper, field[6, x, rows], field[7, x, rows])
                for c in range(3):
                    for m in range(4):
                        forces[x, 4 * c + m, rows] = pushed[c][m] + down[c][m]
                return upper, up

            nothing = [[jnp.zeros((ROWS, LANES), F32) for m in range(4)] for c in range(3)]
            lax.fori_loop(low - 1, high, forces_body, (load_modes(low - 1), nothing))

        def update_body(x, carry, turn=turn, final=final):
            g = lax.div(x, 3)
            i = lax.rem(x, 3)
            rest = []
            for c in range(3):
                stay, go = gather_rows([forces[x, 4 * c + m] for m in range(4)])
                come = jnp.where(first_lane, at_low(strip_push[c, i], g), lane_prev(go))
                rest.append(field[3 + c, x] - (stay + come))
            moved = apply_inverse([inv[k, x] for k in range(6)], rest)
            for c in range(3):
                if final:
                    out_residual[c, x - REACH] = moved[c][:ROWS]
                else:
                    keep, add = weights[turn]
                    change = add * moved[c]
                    if turn > 0:
                        change = keep * step[c, x] + change
                    if turn < 2:
                        step[c, x] = change
                    field[c, x] = field[c, x] + change
            return carry

        lax.fori_loop(low, high, update_body, 0)
        if turn == 2:
            for c in range(3):
                out_solution[c] = field[c, REACH : REACH + layers, :ROWS]


def vmem(count):
    return [pl.BlockSpec(memory_space=pltpu.VMEM)] * count


def tiles(*lead):
    return jax.ShapeDtypeStruct((*lead, ROWS, LANES), F32)


def solution(mesh):
    dims = tuple(mesh.shape[axis] for axis in AXES)

    def swap(value, axis, kind):
        return lax.ppermute(value, AXES, swap_pairs(dims, axis, kind))

    def body(forcing, guess, lame, shear):
        layers = lame.shape[0]
        wide = layers + 2 * REACH
        params = pltpu.CompilerParams(vmem_limit_bytes=32 * 1024 * 1024)
        own, z_near, z_far, y0_near, y0_far, x_near, x_far = pl.pallas_call(
            pack_first,
            out_shape=[tiles(layers)] + [tiles(layers // 4)] * 2 + [tiles(4 * layers)] * 2 + [tiles(X_TILES)] * 2,
            in_specs=vmem(4),
            out_specs=vmem(7),
            compiler_params=params,
            name="pack_first",
        )(forcing, guess, lame, shear)
        z_far = swap(z_far, 2, 1)
        z_near = swap(z_near, 2, 0)
        y0_near = swap(y0_near, 1, 0)
        y0_far = swap(y0_far, 1, 1)
        full, x_near, x_far = pl.pallas_call(
            pack_second,
            out_shape=[tiles(layers), tiles(X_TILES), tiles(X_TILES)],
            in_specs=vmem(5),
            out_specs=vmem(3),
            compiler_params=params,
            name="pack_second",
        )(own, z_near, z_far, x_near, x_far)
        x_near = swap(x_near, 0, 0)
        x_far = swap(x_far, 0, 1)
        y1_near, y1_far = pl.pallas_call(
            pack_third,
            out_shape=[tiles(X_TILES + layers // 2)] * 2,
            in_specs=vmem(3),
            out_specs=vmem(2),
            compiler_params=params,
            name="pack_third",
        )(full, x_near, x_far)
        y1_near = swap(y1_near, 1, 0)
        y1_far = swap(y1_far, 1, 1)
        block = (2 * ROWS, LANES)
        return pl.pallas_call(
            smooth,
            out_shape=[tiles(3, layers), tiles(3, layers)],
            in_specs=vmem(11),
            out_specs=vmem(2),
            scratch_shapes=[
                pltpu.VMEM((8, wide, *block), F32),
                pltpu.VMEM((wide, *block), F32),
                pltpu.VMEM((8, 3, *block), F32),
                pltpu.VMEM((6, 3, *block), F32),
                pltpu.VMEM((3, 3, *block), F32),
                pltpu.VMEM((3, 3, *block), F32),
                pltpu.VMEM((6, wide, *block), F32),
                pltpu.VMEM((3, wide, *block), F32),
                pltpu.VMEM((wide, 12, *block), F32),
                pltpu.VMEM((wide, 12, *block), F32),
            ],
            compiler_params=params,
            name="smooth",
        )(forcing, guess, lame, shear, full, y0_near, y0_far, x_near, x_far, y1_near, y1_far)

    in_specs = (P(None, *AXES), P(None, *AXES), P(*AXES), P(*AXES))
    out_specs = (P(None, *AXES), P(None, *AXES))
    return jax.shard_map(body, mesh=mesh, in_specs=in_specs, out_specs=out_specs, check_vma=False)
```

```python
import itertools

import jax
import jax.numpy as jnp
from jax import lax
from jax.experimental import pallas as pl
from jax.experimental.pallas import tpu as pltpu
from jax.sharding import PartitionSpec as P

AXES = ("gx", "gy", "gz")
REACH = 4
F32 = jnp.float32
LANES = 128
TOGETHER = 6
FIRST_TOGETHER = 8
INVERSE_TOGETHER = 11
FORCES_TOGETHER = 4
ROWS = 8


def swap_pairs(dims, axis, kind):
    other = (1, 0, 1)[axis]

    def place(spot):
        return (spot[0] * dims[1] + spot[1]) * dims[2] + spot[2]

    pairs = []
    for spot in itertools.product(*(range(size) for size in dims)):
        goal = list(spot)
        mate = (spot[axis] ^ 1) if kind == 0 else ((spot[axis] + 1) ^ 1) - 1
        if 0 <= mate < dims[axis]:
            goal[axis] = mate
        else:
            goal[other] ^= 1
        pairs.append((place(spot), place(goal)))
    return pairs


def iota(shape, dim):
    return lax.broadcasted_iota(jnp.int32, shape, dim)


def half_turn(tile):
    return pltpu.roll(tile, ROWS // 2, 0)


def even(axis):
    return lax.rem(lax.axis_index(axis), 2) == 0


def at_end(axis):
    place = lax.axis_index(axis)
    return jnp.logical_or(place == 0, place == lax.axis_size(axis) - 1)


def fields_of(forcing, guess, lame, shear):
    return [guess.at[c] for c in range(3)] + [forcing.at[c] for c in range(3)] + [lame, shear]


def row_mask(flag):
    low = iota((ROWS, LANES), 0) < ROWS // 2
    return jnp.logical_xor(low, jnp.broadcast_to(flag, low.shape))


X_LAYERS = (4, 4, 4, 3, 3, 3, 4, 4, 4)
X_STARTS = tuple(sum(X_LAYERS[:f]) for f in range(9))
X_TILES = sum(X_LAYERS)


def pack_first(
    forcing_hbm, guess_hbm, lame_hbm, shear_hbm, own, z_near, z_far, y_near, y_far, x_near, x_far,
    forcing, guess, lame, shear, arrived,
):
    pairs = ((forcing_hbm, forcing), (guess_hbm, guess), (lame_hbm, lame), (shear_hbm, shear))
    copies = [pltpu.make_async_copy(*pair, arrived.at[i]) for i, pair in enumerate(pairs)]
    for copy in copies:
        copy.start()
    for copy in copies:
        copy.wait()
    fields = fields_of(forcing, guess, lame, shear)
    layers = own.shape[0]
    slot = lax.rem(iota((ROWS, LANES), 1), 16)
    group = lax.div(iota((ROWS, LANES), 1), 16)
    quarter = lax.div(slot, 4)
    edges = []
    for x in range(layers):
        low = jnp.zeros((ROWS, LANES), F32)
        high = low
        for f in range(8):
            tile = fields[f][x]
            low = jnp.where(group == f, pltpu.roll(tile, (16 * f + 4) % LANES, 1), low)
            high = jnp.where(group == f, pltpu.roll(tile, (16 * f + 12) % LANES, 1), high)
        tile = jnp.where(slot < 8, low, high)
        own[x] = tile
        edges.append(tile)
    up_first = even("gz")
    quads = layers // 4
    for q in range(quads):
        up = edges[q]
        down = edges[q]
        for j in range(4):
            tile = edges[q + quads * j]
            up = jnp.where(quarter == j, pltpu.roll(tile, (4 * j - 8) % LANES, 1), up)
            down = jnp.where(quarter == j, pltpu.roll(tile, (4 * j - 4) % LANES, 1), down)
        z_near[q] = jnp.where(up_first, up, down)
        z_far[q] = jnp.where(up_first, down, up)
    keep = row_mask(even("gy"))
    half = layers // 2
    for f in range(8):
        for x in range(half):
            here = fields[f][x]
            there = half_turn(fields[f][x + half])
            y_near[f * half + x] = jnp.where(keep, here, there)
            y_far[f * half + x] = jnp.where(keep, there, here)
    up_first = even("gx")
    for f in range(8):
        count = X_LAYERS[f]
        last = layers - count
        for x in range(count):
            x_near[X_STARTS[f] + x] = fields[f][jnp.where(up_first, last, 0) + x]
            x_far[X_STARTS[f] + x] = fields[f][jnp.where(up_first, 0, last) + x]


def pack_second(own, z_near, z_far, x_near_in, x_far_in, full, x_near, x_far):
    layers = own.shape[0]
    filled = pl.ds(0, X_STARTS[8])
    x_near[filled] = x_near_in[filled]
    x_far[filled] = x_far_in[filled]
    quads = layers // 4
    slot = lax.rem(iota((ROWS, LANES), 1), 16)
    forward = even("gz")
    ends = at_end("gz")
    for q in range(quads):
        near = z_near[q]
        far = jnp.where(ends, 0.0, z_far[q])
        behind = jnp.where(forward, far, near)
        ahead = jnp.where(forward, near, far)
        for j in range(4):
            x = q + quads * j
            tile = jnp.where(slot < 4, pltpu.roll(behind, (-4 * j) % LANES, 1), own[x])
            full[x] = jnp.where(slot >= 12, pltpu.roll(ahead, (12 - 4 * j) % LANES, 1), tile)
    up_first = even("gx")
    last = layers - 4
    for x in range(4):
        x_near[X_STARTS[8] + x] = full[jnp.where(up_first, last, 0) + x]
        x_far[X_STARTS[8] + x] = full[jnp.where(up_first, 0, last) + x]


def pack_third(full, x_near, x_far, y_near, y_far):
    keep = row_mask(even("gy"))
    half = full.shape[0] // 2
    for i in range(X_TILES):
        here = x_near[i]
        there = half_turn(x_far[i])
        y_near[i] = jnp.where(keep, here, there)
        y_far[i] = jnp.where(keep, there, here)
    for x in range(half):
        here = full[x]
        there = half_turn(full[x + half])
        y_near[X_TILES + x] = jnp.where(keep, here, there)
        y_far[X_TILES + x] = jnp.where(keep, there, here)


def row_next(tile):
    return pltpu.roll(tile, tile.shape[0] - 1, 0)


def row_prev(tile):
    return pltpu.roll(tile, 1, 0)


def lane_next(tile):
    return pltpu.roll(tile, LANES - 1, 1)


def lane_prev(tile):
    return pltpu.roll(tile, 1, 1)


def node_modes(here, beyond):
    total = here + beyond
    change = beyond - here
    total_y = row_next(total)
    change_y = row_next(change)
    return (total + total_y, total_y - total, change + change_y, change_y - change)


def element_modes(lower, upper, lam, mu):
    s = [[lower[c][m] + upper[c][m] for m in range(4)] for c in range(3)]
    d = [[upper[c][m] - lower[c][m] for m in range(4)] for c in range(3)]
    mu2 = mu + mu
    lam3 = lam * (1.0 / 3.0)
    mu3 = mu * (1.0 / 3.0)
    stiff = (lam3 + 4.0 * mu3) * (1.0 / 3.0)
    pressure = lam * (d[0][0] + s[1][1] + s[2][2])
    xx = pressure + mu2 * d[0][0]
    yy = pressure + mu2 * s[1][1]
    zz = pressure + mu2 * s[2][2]
    xy = mu * (s[0][1] + d[1][0])
    xz = mu * (s[0][2] + d[2][0])
    yz = mu * (s[1][2] + s[2][1])
    along_y = lam3 * (d[0][1] + s[2][3])
    along_z = lam3 * (d[0][2] + s[1][3])
    along_x = lam3 * (d[1][1] + d[2][2])
    twist = mu3 * (s[0][3] + d[1][2] + d[2][1])
    fs = [
        [None, xy, xz, twist + mu3 * s[0][3]],
        [None, yy, yz, along_z + mu * s[1][3]],
        [None, yz, zz, along_y + mu * s[2][3]],
    ]
    fd = [
        [xx, along_y + mu * d[0][1], along_z + mu * d[0][2], stiff * d[0][3]],
        [xy, along_x + mu * d[1][1], twist + mu3 * d[1][2], stiff * d[1][3]],
        [xz, twist + mu3 * d[2][1], along_x + mu * d[2][2], stiff * d[2][3]],
    ]
    low = [[-fd[c][0]] + [fs[c][m] - fd[c][m] for m in range(1, 4)] for c in range(3)]
    high = [[fd[c][0]] + [fs[c][m] + fd[c][m] for m in range(1, 4)] for c in range(3)]
    return low, high


def gather_rows(modes):
    total = (modes[0] - modes[1]) + row_prev(modes[0] + modes[1])
    change = (modes[2] - modes[3]) + row_prev(modes[2] + modes[3])
    return total - change, total + change


def apply_inverse(inv, vec):
    return (
        inv[0] * vec[0] + inv[1] * vec[1] + inv[2] * vec[2],
        inv[1] * vec[0] + inv[3] * vec[1] + inv[4] * vec[2],
        inv[2] * vec[0] + inv[4] * vec[1] + inv[5] * vec[2],
    )


def block_parts(lam, mu, shift):
    stiff = lam + 4.0 * mu
    cross = lam + mu
    stiff = stiff + shift[0](stiff)
    behind = shift[1](cross)
    total = behind + cross
    change = behind - cross
    total_y = row_prev(total)
    change_y = row_prev(change)
    return (stiff + row_prev(stiff), total_y - total, change_y + change, change_y - change)


def block_inverse(before, after, valid):
    diag = (16.0 / 9.0) * (before[0] + after[0])
    p = (4.0 / 3.0) * (before[1] - after[1])
    q = (4.0 / 3.0) * (before[2] - after[2])
    s = (4.0 / 3.0) * (before[3] + after[3])
    c00 = diag * diag - s * s
    c01 = q * s - p * diag
    c02 = p * s - q * diag
    scale = 1.0 / (diag * c00 + p * c01 + q * c02)
    cof = (c00, c01, c02, diag * diag - q * q, p * q - diag * s, diag * diag - p * p)
    return [jnp.where(valid, entry * scale, 0.0) for entry in cof]


def sweep(low, high, body, carry, together):
    whole = (high - low) // together

    def many(trip, carry):
        for i in range(together):
            carry = body(low + trip * together + i, carry)
        return carry

    carry = lax.fori_loop(0, whole, many, carry)
    for x in range(low + whole * together, high):
        carry = body(x, carry)
    return carry


def step_weights():
    low, high = (0.3, 3.0)
    theta = (high + low) / 2.0
    delta = (high - low) / 2.0
    sigma = theta / delta
    weights = [(0.0, 1.0 / theta)]
    rho_old = 1.0 / sigma
    for _ in range(2):
        rho = 1.0 / (2.0 * sigma - rho_old)
        weights.append((rho * rho_old, 2.0 * rho / delta))
        rho_old = rho
    return weights


def smooth(
    forcing, guess, lame, shear, full, y0_near, y0_far, x_near, x_far, y1_near, y1_far,
    out_solution, out_residual,
    field, edge, strip, strip_inv, strip_step, strip_push, inv, step, modes, forces,
):
    own_fields = fields_of(forcing, guess, lame, shear)
    layers = full.shape[0]
    wide = layers + 2 * REACH
    half = layers // 2
    tall = 2 * ROWS

    y_keep = row_mask(jnp.logical_not(even("gy")))
    y_ends = at_end("gy")
    x_forward = even("gx")
    x_ends = at_end("gx")

    def scaled(f, tile):
        return tile * (1.0 / 16.0) if f in (6, 7) else tile

    def beside(near, far):
        far = jnp.where(y_ends, 0.0, far)
        return jnp.where(y_keep, near, far), half_turn(jnp.where(y_keep, far, near))

    def target(f):
        return field.at[f] if f < 8 else edge

    zero = jnp.zeros((tall, LANES), F32)
    for f in range(3, 6):
        field[f, 0] = zero
        field[f, wide - 1] = zero
    for f in range(9):
        for x in range(half):
            if f < 8:
                i = f * half + x
                first, second = beside(y0_near[i], y0_far[i])
                target(f)[REACH + x, :ROWS] = scaled(f, own_fields[f][x])
                target(f)[REACH + x + half, :ROWS] = scaled(f, own_fields[f][x + half])
            else:
                i = X_TILES + x
                first, second = beside(y1_near[i], y1_far[i])
                edge[REACH + x, :ROWS] = full[x]
                edge[REACH + x + half, :ROWS] = full[x + half]
            target(f)[REACH + x, ROWS:] = scaled(f, first)
            target(f)[REACH + x + half, ROWS:] = scaled(f, second)
    for f in range(9):
        count = X_LAYERS[f]
        ahead = REACH + layers
        behind = REACH - count
        to_near = jnp.where(x_forward, ahead, behind)
        to_far = jnp.where(x_forward, behind, ahead)
        for x in range(count):
            i = X_STARTS[f] + x
            target(f)[to_near + x, :ROWS] = scaled(f, x_near[i])
            target(f)[to_far + x, :ROWS] = jnp.where(x_ends, 0.0, scaled(f, x_far[i]))
            first, second = beside(y1_near[i], y1_far[i])
            target(f)[to_near + x, ROWS:] = scaled(f, first)
            target(f)[to_far + x, ROWS:] = jnp.where(x_ends, 0.0, scaled(f, second))

    lane = iota((tall, LANES), 1)
    row = iota((tall, LANES), 0)
    group = lax.div(lane, 16)
    slot = lax.rem(lane, 16)
    first_lane = lane == 0
    last_lane = lane == LANES - 1

    groups = wide // 3
    for i in range(3):
        for f in range(8):
            tile = zero
            for g in range(groups):
                moved = pltpu.roll(edge[3 * g + i], (16 * (g - f)) % LANES, 1)
                tile = jnp.where(group == g, moved, tile)
            strip[f, i] = scaled(f, tile)

    place_x, place_y, place_z = (lax.axis_index(axis) for axis in AXES)
    count_x, count_y, count_z = (lax.axis_size(axis) for axis in AXES)
    from_x = jnp.where(place_x == 0, REACH, 0)
    to_x = jnp.where(place_x == count_x - 1, REACH + layers, wide)
    row_from = jnp.where(place_y == count_y - 1, ROWS + 4, ROWS)
    row_to = jnp.where(place_y == 0, ROWS + 4, tall)
    row_ok = jnp.logical_or(row < ROWS, jnp.logical_and(row >= row_from, row < row_to))
    slot_from = jnp.where(place_z == 0, 4, 0)
    slot_to = jnp.where(place_z == count_z - 1, 12, 16)
    slot_ok = jnp.logical_and(row_ok, jnp.logical_and(slot >= slot_from, slot < slot_to))

    def strip_next(tiles):
        return [tiles[1], tiles[2], pltpu.roll(tiles[0], LANES - 16, 1)]

    def strip_prev(tiles):
        return [pltpu.roll(tiles[2], 16, 1), tiles[0], tiles[1]]

    def at_high(tile, g):
        return pltpu.roll(tile, lax.rem(LANES + 115 - 16 * g, LANES), 1)

    def at_low(tile, g):
        return pltpu.roll(tile, lax.rem(LANES + 125 - 16 * g, LANES), 1)

    parts = [block_parts(strip[6, i], strip[7, i], (lane_prev, lane_prev)) for i in range(3)]
    previous = [strip_prev([parts[i][k] for i in range(3)]) for k in range(4)]
    for i in range(3):
        layer = 3 * group + i
        valid = jnp.logical_and(slot_ok, jnp.logical_and(layer >= from_x, layer < to_x))
        entries = block_inverse([previous[k][i] for k in range(4)], parts[i], valid)
        for k in range(6):
            strip_inv[k, i] = entries[k]

    def main_parts(x):
        g = lax.div(x, 3)
        i = lax.rem(x, 3)
        lam_low = at_low(strip[6, i], g)
        mu_low = at_low(strip[7, i], g)

        def shift_stiff(tile):
            return jnp.where(first_lane, lam_low + 4.0 * mu_low, lane_prev(tile))

        def shift_cross(tile):
            return jnp.where(first_lane, lam_low + mu_low, lane_prev(tile))

        return block_parts(field[6, x], field[7, x], (shift_stiff, shift_cross))

    def inverse_body(x, before):
        after = main_parts(x)
        valid = jnp.logical_and(row_ok, jnp.logical_and(x >= from_x, x < to_x))
        entries = block_inverse(before, after, valid)
        for k in range(6):
            inv[k, x] = entries[k]
        return after

    sweep(1, wide - 1, inverse_body, main_parts(0), INVERSE_TOGETHER)

    def place_of(x):
        return lax.div(x, 3), lax.rem(x, 3)

    def modes_of(tiles, high_edges):
        return [
            node_modes(tiles[c], jnp.where(last_lane, high_edges[c], lane_next(tiles[c]))) for c in range(3)
        ]

    def high_edges_of(x):
        g, i = place_of(x)
        return [at_high(strip[c, i], g) for c in range(3)]

    def store_modes(x, values):
        for c in range(3):
            for m in range(4):
                modes[x, 4 * c + m] = values[c][m]

    def first_modes(trip, carry):
        spots = [FIRST_TOGETHER * trip + i for i in range(FIRST_TOGETHER)]
        loaded = [([field[c, x] for c in range(3)], high_edges_of(x)) for x in spots]
        values = [modes_of(*pair) for pair in loaded]
        for x, value in zip(spots, values):
            store_modes(x, value)
        return carry

    lax.fori_loop(0, wide // FIRST_TOGETHER, first_modes, 0)

    weights = step_weights()
    for turn in range(4):
        final = turn == 3
        here = [[strip[c, i] for i in range(3)] for c in range(3)]
        node = [[node_modes(here[c][i], lane_next(here[c][i])) for c in range(3)] for i in range(3)]
        above = [[[None] * 4 for c in range(3)] for i in range(3)]
        for c in range(3):
            for m in range(4):
                moved = strip_next([node[i][c][m] for i in range(3)])
                for i in range(3):
                    above[i][c][m] = moved[i]
        push = [element_modes(node[i], above[i], strip[6, i], strip[7, i]) for i in range(3)]
        pull = [[None] * 3 for i in range(3)]
        for c in range(3):
            total = [[None] * 4 for i in range(3)]
            for m in range(4):
                moved = strip_prev([push[i][1][c][m] for i in range(3)])
                for i in range(3):
                    total[i][m] = moved[i] + push[i][0][c][m]
            for i in range(3):
                stay, go = gather_rows(total[i])
                strip_push[c, i] = go
                pull[i][c] = stay + lane_prev(go)

        low, high = 1 + turn, wide - 1 - turn

        if not final:
            keep, add = weights[turn]
            for i in range(3):
                rest = [strip[3 + c, i] - pull[i][c] for c in range(3)]
                moved = apply_inverse([strip_inv[k, i] for k in range(6)], rest)
                for c in range(3):
                    change = add * moved[c]
                    if turn > 0:
                        change = keep * strip_step[c, i] + change
                    strip_step[c, i] = change
                    strip[c, i] = strip[c, i] + change

        for part in range(2):
            rows = pl.ds(part * ROWS, ROWS)

            def load_modes(x, rows=rows):
                return [[modes[x, 4 * c + m, rows] for m in range(4)] for c in range(3)]

            def forces_body(x, carry, rows=rows, load_modes=load_modes):
                lower, pushed = carry
                upper = load_modes(x + 1)
                down, up = element_modes(lower, upper, field[6, x, rows], field[7, x, rows])
                for c in range(3):
                    for m in range(4):
                        forces[x, 4 * c + m, rows] = pushed[c][m] + down[c][m]
                return upper, up

            nothing = [[jnp.zeros((ROWS, LANES), F32) for m in range(4)] for c in range(3)]
            sweep(low - 1, high, forces_body, (load_modes(low - 1), nothing), FORCES_TOGETHER)

        def update_layers(spots, turn=turn, final=final):
            loaded = []
            for x in spots:
                g, i = place_of(x)
                loaded.append(
                    (
                        [[forces[x, 4 * c + m] for m in range(4)] for c in range(3)],
                        [at_low(strip_push[c, i], g) for c in range(3)],
                        [field[3 + c, x] for c in range(3)],
                        [inv[k, x] for k in range(6)],
                        None if final else [field[c, x] for c in range(3)],
                        [step[c, x] for c in range(3)] if 0 < turn < 3 else None,
                        None if final else high_edges_of(x),
                    )
                )
            results = []
            for force, come, load, block, value, before, high_edges in loaded:
                rest = []
                for c in range(3):
                    stay, go = gather_rows(force[c])
                    rest.append(load[c] - (stay + jnp.where(first_lane, come[c], lane_prev(go))))
                if final:
                    moved = apply_inverse([entry[:ROWS] for entry in block], [part[:ROWS] for part in rest])
                    results.append((moved, None, None))
                    continue
                keep, add = weights[turn]
                moved = [add * part for part in apply_inverse(block, rest)]
                if turn > 0:
                    moved = [keep * before[c] + moved[c] for c in range(3)]
                value = [value[c] + moved[c] for c in range(3)]
                results.append((moved, value, modes_of(value, high_edges)))
            for x, (moved, value, onward) in zip(spots, results):
                for c in range(3):
                    if final:
                        out_residual[c, x - REACH] = moved[c]
                    else:
                        if turn < 2:
                            step[c, x] = moved[c]
                        field[c, x] = value[c]
                if not final:
                    store_modes(x, onward)

        def update_body(trip, carry, low=low, update_layers=update_layers):
            update_layers([low + TOGETHER * trip + i for i in range(TOGETHER)])
            return carry

        trips = (high - low) // TOGETHER
        lax.fori_loop(0, trips, update_body, 0)
        if low + TOGETHER * trips < high:
            update_layers(list(range(low + TOGETHER * trips, high)))
        if turn == 2:
            for c in range(3):
                out_solution[c] = field[c, REACH : REACH + layers, :ROWS]


def vmem(count):
    return [pl.BlockSpec(memory_space=pltpu.VMEM)] * count


def tiles(*lead):
    return jax.ShapeDtypeStruct((*lead, ROWS, LANES), F32)


def solution(mesh):
    dims = tuple(mesh.shape[axis] for axis in AXES)

    def swap(value, axis, kind):
        return lax.ppermute(value, AXES, swap_pairs(dims, axis, kind))

    def body(forcing, guess, lame, shear):
        layers = lame.shape[0]
        wide = layers + 2 * REACH
        params = pltpu.CompilerParams(vmem_limit_bytes=32 * 1024 * 1024)
        own, z_near, z_far, y0_near, y0_far, x_near, x_far = pl.pallas_call(
            pack_first,
            out_shape=[tiles(layers)] + [tiles(layers // 4)] * 2 + [tiles(4 * layers)] * 2 + [tiles(X_TILES)] * 2,
            in_specs=[pl.BlockSpec(memory_space=pltpu.HBM)] * 4,
            out_specs=vmem(7),
            scratch_shapes=[pltpu.VMEM(a.shape, F32) for a in (forcing, guess, lame, shear)]
            + [pltpu.SemaphoreType.DMA((4,))],
            compiler_params=params,
            name="pack_first",
        )(*(pltpu.with_memory_space_constraint(a, pltpu.HBM) for a in (forcing, guess, lame, shear)))
        z_far = swap(z_far, 2, 1)
        z_near = swap(z_near, 2, 0)
        y0_near = swap(y0_near, 1, 0)
        y0_far = swap(y0_far, 1, 1)
        full, x_near, x_far = pl.pallas_call(
            pack_second,
            out_shape=[tiles(layers), tiles(X_TILES), tiles(X_TILES)],
            in_specs=vmem(5),
            out_specs=vmem(3),
            compiler_params=params,
            name="pack_second",
        )(own, z_near, z_far, x_near, x_far)
        x_near = swap(x_near, 0, 0)
        x_far = swap(x_far, 0, 1)
        y1_near, y1_far = pl.pallas_call(
            pack_third,
            out_shape=[tiles(X_TILES + layers // 2)] * 2,
            in_specs=vmem(3),
            out_specs=vmem(2),
            compiler_params=params,
            name="pack_third",
        )(full, x_near, x_far)
        y1_near = swap(y1_near, 1, 0)
        y1_far = swap(y1_far, 1, 1)
        block = (2 * ROWS, LANES)
        return pl.pallas_call(
            smooth,
            out_shape=[tiles(3, layers), tiles(3, layers)],
            in_specs=vmem(11),
            out_specs=vmem(2),
            scratch_shapes=[
                pltpu.VMEM((8, wide, *block), F32),
                pltpu.VMEM((wide, *block), F32),
                pltpu.VMEM((8, 3, *block), F32),
                pltpu.VMEM((6, 3, *block), F32),
                pltpu.VMEM((3, 3, *block), F32),
                pltpu.VMEM((3, 3, *block), F32),
                pltpu.VMEM((6, wide, *block), F32),
                pltpu.VMEM((3, wide, *block), F32),
                pltpu.VMEM((wide, 12, *block), F32),
                pltpu.VMEM((wide, 12, *block), F32),
            ],
            compiler_params=params,
            name="smooth",
        )(forcing, guess, lame, shear, full, y0_near, y0_far, x_near, x_far, y1_near, y1_far)

    in_specs = (P(None, *AXES), P(None, *AXES), P(*AXES), P(*AXES))
    out_specs = (P(None, *AXES), P(None, *AXES))
    return jax.shard_map(body, mesh=mesh, in_specs=in_specs, out_specs=out_specs, check_vma=False)
```

```python
import itertools

import jax
import jax.numpy as jnp
from jax import lax
from jax.experimental import pallas as pl
from jax.experimental.pallas import tpu as pltpu
from jax.sharding import PartitionSpec as P

AXES = ("gx", "gy", "gz")
REACH = 4
F32 = jnp.float32
LANES = 128
TOGETHER = 6
FIRST_TOGETHER = 8
INVERSE_TOGETHER = 11
FORCES_TOGETHER = 4
ROWS = 8


def swap_pairs(dims, axis, kind):
    other = (1, 0, 1)[axis]

    def place(spot):
        return (spot[0] * dims[1] + spot[1]) * dims[2] + spot[2]

    pairs = []
    for spot in itertools.product(*(range(size) for size in dims)):
        goal = list(spot)
        mate = (spot[axis] ^ 1) if kind == 0 else ((spot[axis] + 1) ^ 1) - 1
        if 0 <= mate < dims[axis]:
            goal[axis] = mate
        else:
            goal[other] ^= 1
        pairs.append((place(spot), place(goal)))
    return pairs


def iota(shape, dim):
    return lax.broadcasted_iota(jnp.int32, shape, dim)


def half_turn(tile):
    return pltpu.roll(tile, ROWS // 2, 0)


def even(axis):
    return lax.rem(lax.axis_index(axis), 2) == 0


def at_end(axis):
    place = lax.axis_index(axis)
    return jnp.logical_or(place == 0, place == lax.axis_size(axis) - 1)


def fields_of(forcing, guess, lame, shear):
    return [guess.at[c] for c in range(3)] + [forcing.at[c] for c in range(3)] + [lame, shear]


def row_mask(flag):
    low = iota((ROWS, LANES), 0) < ROWS // 2
    return jnp.logical_xor(low, jnp.broadcast_to(flag, low.shape))


X_LAYERS = (4, 4, 4, 3, 3, 3, 4, 4, 4)
X_STARTS = tuple(sum(X_LAYERS[:f]) for f in range(9))
X_TILES = sum(X_LAYERS)


def pack_first(forcing_hbm, guess_hbm, lame_hbm, shear_hbm, forcing, guess, lame, shear, own, z_near, z_far, arrived):
    pairs = ((forcing_hbm, forcing), (guess_hbm, guess), (lame_hbm, lame), (shear_hbm, shear))
    copies = [pltpu.make_async_copy(*pair, arrived.at[i]) for i, pair in enumerate(pairs)]
    for copy in copies:
        copy.start()
    for copy in copies:
        copy.wait()
    fields = fields_of(forcing, guess, lame, shear)
    layers = own.shape[0]
    slot = lax.rem(iota((ROWS, LANES), 1), 16)
    group = lax.div(iota((ROWS, LANES), 1), 16)
    quarter = lax.div(slot, 4)
    edges = []
    for x in range(layers):
        low = jnp.zeros((ROWS, LANES), F32)
        high = low
        for f in range(8):
            tile = fields[f][x]
            low = jnp.where(group == f, pltpu.roll(tile, (16 * f + 4) % LANES, 1), low)
            high = jnp.where(group == f, pltpu.roll(tile, (16 * f + 12) % LANES, 1), high)
        tile = jnp.where(slot < 8, low, high)
        own[x] = tile
        edges.append(tile)
    up_first = even("gz")
    quads = layers // 4
    for q in range(quads):
        up = edges[q]
        down = edges[q]
        for j in range(4):
            tile = edges[q + quads * j]
            up = jnp.where(quarter == j, pltpu.roll(tile, (4 * j - 8) % LANES, 1), up)
            down = jnp.where(quarter == j, pltpu.roll(tile, (4 * j - 4) % LANES, 1), down)
        z_near[q] = jnp.where(up_first, up, down)
        z_far[q] = jnp.where(up_first, down, up)


def pack_rest(forcing, guess, lame, shear, y_near, y_far, x_near, x_far):
    fields = fields_of(forcing, guess, lame, shear)
    layers = lame.shape[0]
    keep = row_mask(even("gy"))
    half = layers // 2
    for f in range(8):
        for x in range(half):
            here = fields[f][x]
            there = half_turn(fields[f][x + half])
            y_near[f * half + x] = jnp.where(keep, here, there)
            y_far[f * half + x] = jnp.where(keep, there, here)
    up_first = even("gx")
    for f in range(8):
        count = X_LAYERS[f]
        last = layers - count
        for x in range(count):
            x_near[X_STARTS[f] + x] = fields[f][jnp.where(up_first, last, 0) + x]
            x_far[X_STARTS[f] + x] = fields[f][jnp.where(up_first, 0, last) + x]


def pack_second(own, z_near, z_far, x_near_in, x_far_in, full, x_near, x_far):
    layers = own.shape[0]
    filled = pl.ds(0, X_STARTS[8])
    x_near[filled] = x_near_in[filled]
    x_far[filled] = x_far_in[filled]
    quads = layers // 4
    slot = lax.rem(iota((ROWS, LANES), 1), 16)
    forward = even("gz")
    ends = at_end("gz")
    for q in range(quads):
        near = z_near[q]
        far = jnp.where(ends, 0.0, z_far[q])
        behind = jnp.where(forward, far, near)
        ahead = jnp.where(forward, near, far)
        for j in range(4):
            x = q + quads * j
            tile = jnp.where(slot < 4, pltpu.roll(behind, (-4 * j) % LANES, 1), own[x])
            full[x] = jnp.where(slot >= 12, pltpu.roll(ahead, (12 - 4 * j) % LANES, 1), tile)
    up_first = even("gx")
    last = layers - 4
    for x in range(4):
        x_near[X_STARTS[8] + x] = full[jnp.where(up_first, last, 0) + x]
        x_far[X_STARTS[8] + x] = full[jnp.where(up_first, 0, last) + x]


def pack_third(full, x_near, x_far, y_near, y_far):
    keep = row_mask(even("gy"))
    half = full.shape[0] // 2
    for i in range(X_TILES):
        here = x_near[i]
        there = half_turn(x_far[i])
        y_near[i] = jnp.where(keep, here, there)
        y_far[i] = jnp.where(keep, there, here)
    for x in range(half):
        here = full[x]
        there = half_turn(full[x + half])
        y_near[X_TILES + x] = jnp.where(keep, here, there)
        y_far[X_TILES + x] = jnp.where(keep, there, here)


def turn_rows(tile, shift, seam):
    first = pltpu.roll(tile[:ROWS], shift, 0)
    second = pltpu.roll(tile[ROWS:], shift, 0)
    crossing = iota((ROWS, LANES), 0) == seam
    return jnp.concatenate([jnp.where(crossing, second, first), jnp.where(crossing, first, second)], 0)


def row_next(tile):
    return turn_rows(tile, ROWS - 1, ROWS - 1)


def row_prev(tile):
    return turn_rows(tile, 1, 0)


def lane_next(tile):
    return pltpu.roll(tile, LANES - 1, 1)


def lane_prev(tile):
    return pltpu.roll(tile, 1, 1)


def node_modes(here, beyond):
    total = here + beyond
    change = beyond - here
    total_y = row_next(total)
    change_y = row_next(change)
    return (total + total_y, total_y - total, change + change_y, change_y - change)


def element_modes(lower, upper, lam, mu):
    s = [[lower[c][m] + upper[c][m] for m in range(4)] for c in range(3)]
    d = [[upper[c][m] - lower[c][m] for m in range(4)] for c in range(3)]
    mu2 = mu + mu
    lam3 = lam * (1.0 / 3.0)
    mu3 = mu * (1.0 / 3.0)
    stiff = (lam3 + 4.0 * mu3) * (1.0 / 3.0)
    pressure = lam * (d[0][0] + s[1][1] + s[2][2])
    xx = pressure + mu2 * d[0][0]
    yy = pressure + mu2 * s[1][1]
    zz = pressure + mu2 * s[2][2]
    xy = mu * (s[0][1] + d[1][0])
    xz = mu * (s[0][2] + d[2][0])
    yz = mu * (s[1][2] + s[2][1])
    along_y = lam3 * (d[0][1] + s[2][3])
    along_z = lam3 * (d[0][2] + s[1][3])
    along_x = lam3 * (d[1][1] + d[2][2])
    twist = mu3 * (s[0][3] + d[1][2] + d[2][1])
    fs = [
        [None, xy, xz, twist + mu3 * s[0][3]],
        [None, yy, yz, along_z + mu * s[1][3]],
        [None, yz, zz, along_y + mu * s[2][3]],
    ]
    fd = [
        [xx, along_y + mu * d[0][1], along_z + mu * d[0][2], stiff * d[0][3]],
        [xy, along_x + mu * d[1][1], twist + mu3 * d[1][2], stiff * d[1][3]],
        [xz, twist + mu3 * d[2][1], along_x + mu * d[2][2], stiff * d[2][3]],
    ]
    low = [[-fd[c][0]] + [fs[c][m] - fd[c][m] for m in range(1, 4)] for c in range(3)]
    high = [[fd[c][0]] + [fs[c][m] + fd[c][m] for m in range(1, 4)] for c in range(3)]
    return low, high


def gather_rows(modes):
    total = (modes[0] - modes[1]) + row_prev(modes[0] + modes[1])
    change = (modes[2] - modes[3]) + row_prev(modes[2] + modes[3])
    return total - change, total + change


def apply_inverse(inv, vec):
    return (
        inv[0] * vec[0] + inv[1] * vec[1] + inv[2] * vec[2],
        inv[1] * vec[0] + inv[3] * vec[1] + inv[4] * vec[2],
        inv[2] * vec[0] + inv[4] * vec[1] + inv[5] * vec[2],
    )


def block_parts(lam, mu, shift):
    stiff = lam + 4.0 * mu
    cross = lam + mu
    stiff = stiff + shift[0](stiff)
    behind = shift[1](cross)
    total = behind + cross
    change = behind - cross
    total_y = row_prev(total)
    change_y = row_prev(change)
    return (stiff + row_prev(stiff), total_y - total, change_y + change, change_y - change)


def block_inverse(before, after, valid):
    diag = (16.0 / 9.0) * (before[0] + after[0])
    p = (4.0 / 3.0) * (before[1] - after[1])
    q = (4.0 / 3.0) * (before[2] - after[2])
    s = (4.0 / 3.0) * (before[3] + after[3])
    c00 = diag * diag - s * s
    c01 = q * s - p * diag
    c02 = p * s - q * diag
    scale = 1.0 / (diag * c00 + p * c01 + q * c02)
    cof = (c00, c01, c02, diag * diag - q * q, p * q - diag * s, diag * diag - p * p)
    return [jnp.where(valid, entry * scale, 0.0) for entry in cof]


def sweep(low, high, body, carry, together):
    whole = (high - low) // together

    def many(trip, carry):
        for i in range(together):
            carry = body(low + trip * together + i, carry)
        return carry

    carry = lax.fori_loop(0, whole, many, carry)
    for x in range(low + whole * together, high):
        carry = body(x, carry)
    return carry


def step_weights():
    low, high = (0.3, 3.0)
    theta = (high + low) / 2.0
    delta = (high - low) / 2.0
    sigma = theta / delta
    weights = [(0.0, 1.0 / theta)]
    rho_old = 1.0 / sigma
    for _ in range(2):
        rho = 1.0 / (2.0 * sigma - rho_old)
        weights.append((rho * rho_old, 2.0 * rho / delta))
        rho_old = rho
    return weights


def smooth(
    forcing, guess, lame, shear, full, y0_near, y0_far, x_near, x_far, y1_near, y1_far,
    out_solution, out_residual,
    field, edge, strip, strip_inv, strip_step, strip_push, joined, inv, step, modes, forces,
):
    own_fields = fields_of(forcing, guess, lame, shear)
    layers = full.shape[0]
    wide = layers + 2 * REACH
    half = layers // 2
    tall = 2 * ROWS

    y_keep = row_mask(jnp.logical_not(even("gy")))
    y_ends = at_end("gy")
    x_forward = even("gx")
    x_ends = at_end("gx")

    def scaled(f, tile):
        return tile * (1.0 / 16.0) if f in (6, 7) else tile

    def beside(near, far):
        far = jnp.where(y_ends, 0.0, far)
        return jnp.where(y_keep, near, far), half_turn(jnp.where(y_keep, far, near))

    def target(f):
        return field.at[f] if f < 8 else edge

    zero = jnp.zeros((tall, LANES), F32)
    for f in range(3, 6):
        field[f, 0] = zero
        field[f, wide - 1] = zero
    for f in range(9):
        for x in range(half):
            if f < 8:
                i = f * half + x
                first, second = beside(y0_near[i], y0_far[i])
                target(f)[REACH + x, :ROWS] = scaled(f, own_fields[f][x])
                target(f)[REACH + x + half, :ROWS] = scaled(f, own_fields[f][x + half])
            else:
                i = X_TILES + x
                first, second = beside(y1_near[i], y1_far[i])
                edge[REACH + x, :ROWS] = full[x]
                edge[REACH + x + half, :ROWS] = full[x + half]
            target(f)[REACH + x, ROWS:] = scaled(f, first)
            target(f)[REACH + x + half, ROWS:] = scaled(f, second)
    for f in range(9):
        count = X_LAYERS[f]
        ahead = REACH + layers
        behind = REACH - count
        to_near = jnp.where(x_forward, ahead, behind)
        to_far = jnp.where(x_forward, behind, ahead)
        for x in range(count):
            i = X_STARTS[f] + x
            target(f)[to_near + x, :ROWS] = scaled(f, x_near[i])
            target(f)[to_far + x, :ROWS] = jnp.where(x_ends, 0.0, scaled(f, x_far[i]))
            first, second = beside(y1_near[i], y1_far[i])
            target(f)[to_near + x, ROWS:] = scaled(f, first)
            target(f)[to_far + x, ROWS:] = jnp.where(x_ends, 0.0, scaled(f, second))

    lane = iota((tall, LANES), 1)
    row = iota((tall, LANES), 0)
    group = lax.div(lane, 16)
    slot = lax.rem(lane, 16)
    first_lane = lane == 0
    last_lane = lane == LANES - 1

    groups = wide // 3

    def choose(tiles):
        chosen = tiles[0]
        for g in range(1, groups):
            chosen = jnp.where(group == g, tiles[g], chosen)
        return chosen

    for i in range(3):
        rows_of = [edge[3 * g + i] for g in range(groups)]
        turned = [
            pltpu.roll(choose([rows_of[(f + d) % groups] for f in range(8)]), 16 * d, 1) if d else choose(rows_of)
            for d in range(groups)
        ]
        for f in range(8):
            strip[f, i] = scaled(f, choose([turned[(g - f) % groups] for g in range(groups)]))

    place_x, place_y, place_z = (lax.axis_index(axis) for axis in AXES)
    count_x, count_y, count_z = (lax.axis_size(axis) for axis in AXES)
    from_x = jnp.where(place_x == 0, REACH, 0)
    to_x = jnp.where(place_x == count_x - 1, REACH + layers, wide)
    row_from = jnp.where(place_y == count_y - 1, ROWS + 4, ROWS)
    row_to = jnp.where(place_y == 0, ROWS + 4, tall)
    row_ok = jnp.logical_or(row < ROWS, jnp.logical_and(row >= row_from, row < row_to))
    slot_from = jnp.where(place_z == 0, 4, 0)
    slot_to = jnp.where(place_z == count_z - 1, 12, 16)
    slot_ok = jnp.logical_and(row_ok, jnp.logical_and(slot >= slot_from, slot < slot_to))

    def strip_next(tiles):
        return [tiles[1], tiles[2], pltpu.roll(tiles[0], LANES - 16, 1)]

    def strip_prev(tiles):
        return [pltpu.roll(tiles[2], 16, 1), tiles[0], tiles[1]]

    def at_high(tile, g):
        return pltpu.roll(tile, lax.rem(LANES + 115 - 16 * g, LANES), 1)

    def at_low(tile, g):
        return pltpu.roll(tile, lax.rem(LANES + 125 - 16 * g, LANES), 1)

    parts = [block_parts(strip[6, i], strip[7, i], (lane_prev, lane_prev)) for i in range(3)]
    previous = [strip_prev([parts[i][k] for i in range(3)]) for k in range(4)]
    for i in range(3):
        layer = 3 * group + i
        valid = jnp.logical_and(slot_ok, jnp.logical_and(layer >= from_x, layer < to_x))
        entries = block_inverse([previous[k][i] for k in range(4)], parts[i], valid)
        for k in range(6):
            strip_inv[k, i] = entries[k]

    def main_parts(x):
        g = lax.div(x, 3)
        i = lax.rem(x, 3)
        lam_low = at_low(strip[6, i], g)
        mu_low = at_low(strip[7, i], g)

        def shift_stiff(tile):
            return jnp.where(first_lane, lam_low + 4.0 * mu_low, lane_prev(tile))

        def shift_cross(tile):
            return jnp.where(first_lane, lam_low + mu_low, lane_prev(tile))

        return block_parts(field[6, x], field[7, x], (shift_stiff, shift_cross))

    def inverse_body(x, before):
        after = main_parts(x)
        valid = jnp.logical_and(row_ok, jnp.logical_and(x >= from_x, x < to_x))
        entries = block_inverse(before, after, valid)
        for k in range(6):
            inv[k, x] = entries[k]
        return after

    sweep(1, wide - 1, inverse_body, main_parts(0), INVERSE_TOGETHER)

    def place_of(x):
        return lax.div(x, 3), lax.rem(x, 3)

    def modes_of(tiles, edges):
        beyond = [
            jnp.where(last_lane, edges[0], lane_next(tiles[0])),
            lane_next(jnp.where(first_lane, edges[0], tiles[1])),
            jnp.where(last_lane, edges[1], lane_next(tiles[2])),
        ]
        return [node_modes(tiles[c], beyond[c]) for c in range(3)]

    def pushed_along(tiles, edges):
        return [
            jnp.where(first_lane, edges[1], lane_prev(tiles[0])),
            lane_prev(jnp.where(last_lane, edges[2], tiles[1])),
            jnp.where(first_lane, edges[2], lane_prev(tiles[2])),
        ]

    def join_edges(push):
        for i in range(3):
            joined[0, i] = jnp.where(slot == 13, pltpu.roll(strip[1, i], 1, 1), strip[0, i])
            if push:
                joined[1, i] = jnp.where(slot == 13, pltpu.roll(strip_push[0, i], 10, 1), strip[2, i])
                last = pltpu.roll(strip_push[2, i], 10, 1)
                joined[2, i] = jnp.where(slot == 13, last, pltpu.roll(strip_push[1, i], 9, 1))
            else:
                joined[1, i] = strip[2, i]

    def edges_of(x, which):
        g, i = place_of(x)
        return [at_high(joined[k, i], g) if k in which else None for k in range(3)]

    join_edges(False)

    def store_modes(x, values):
        for c in range(3):
            for m in range(4):
                modes[x, 4 * c + m] = values[c][m]

    def first_modes(trip, carry):
        spots = [FIRST_TOGETHER * trip + i for i in range(FIRST_TOGETHER)]
        loaded = [([field[c, x] for c in range(3)], edges_of(x, (0, 1))) for x in spots]
        values = [modes_of(*pair) for pair in loaded]
        for x, value in zip(spots, values):
            store_modes(x, value)
        return carry

    lax.fori_loop(0, wide // FIRST_TOGETHER, first_modes, 0)

    weights = step_weights()
    for turn in range(4):
        final = turn == 3
        here = [[strip[c, i] for i in range(3)] for c in range(3)]
        node = [[node_modes(here[c][i], lane_next(here[c][i])) for c in range(3)] for i in range(3)]
        above = [[[None] * 4 for c in range(3)] for i in range(3)]
        for c in range(3):
            for m in range(4):
                moved = strip_next([node[i][c][m] for i in range(3)])
                for i in range(3):
                    above[i][c][m] = moved[i]
        push = [element_modes(node[i], above[i], strip[6, i], strip[7, i]) for i in range(3)]
        pull = [[None] * 3 for i in range(3)]
        for c in range(3):
            total = [[None] * 4 for i in range(3)]
            for m in range(4):
                moved = strip_prev([push[i][1][c][m] for i in range(3)])
                for i in range(3):
                    total[i][m] = moved[i] + push[i][0][c][m]
            for i in range(3):
                stay, go = gather_rows(total[i])
                strip_push[c, i] = go
                pull[i][c] = stay + lane_prev(go)

        low, high = 1 + turn, wide - 1 - turn

        if not final:
            keep, add = weights[turn]
            for i in range(3):
                rest = [strip[3 + c, i] - pull[i][c] for c in range(3)]
                moved = apply_inverse([strip_inv[k, i] for k in range(6)], rest)
                for c in range(3):
                    change = add * moved[c]
                    if turn > 0:
                        change = keep * strip_step[c, i] + change
                    strip_step[c, i] = change
                    strip[c, i] = strip[c, i] + change

        join_edges(True)

        for part in range(2):
            rows = pl.ds(part * ROWS, ROWS)

            def load_modes(x, rows=rows):
                return [[modes[x, 4 * c + m, rows] for m in range(4)] for c in range(3)]

            def forces_body(x, carry, rows=rows, load_modes=load_modes):
                lower, pushed = carry
                upper = load_modes(x + 1)
                down, up = element_modes(lower, upper, field[6, x, rows], field[7, x, rows])
                for c in range(3):
                    for m in range(4):
                        forces[x, 4 * c + m, rows] = pushed[c][m] + down[c][m]
                return upper, up

            nothing = [[jnp.zeros((ROWS, LANES), F32) for m in range(4)] for c in range(3)]
            sweep(low - 1, high, forces_body, (load_modes(low - 1), nothing), FORCES_TOGETHER)

        def update_layers(spots, turn=turn, final=final):
            loaded = []
            for x in spots:
                loaded.append(
                    (
                        [[forces[x, 4 * c + m] for m in range(4)] for c in range(3)],
                        edges_of(x, (1, 2) if final else (0, 1, 2)),
                        [field[3 + c, x] for c in range(3)],
                        [inv[k, x] for k in range(6)],
                        None if final else [field[c, x] for c in range(3)],
                        [step[c, x] for c in range(3)] if 0 < turn < 3 else None,
                    )
                )
            results = []
            for force, edges, load, block, value, before in loaded:
                gathered = [gather_rows(force[c]) for c in range(3)]
                come = pushed_along([go for stay, go in gathered], edges)
                rest = [load[c] - (gathered[c][0] + come[c]) for c in range(3)]
                if final:
                    moved = apply_inverse([entry[:ROWS] for entry in block], [part[:ROWS] for part in rest])
                    results.append((moved, None, None))
                    continue
                keep, add = weights[turn]
                moved = [add * part for part in apply_inverse(block, rest)]
                if turn > 0:
                    moved = [keep * before[c] + moved[c] for c in range(3)]
                value = [value[c] + moved[c] for c in range(3)]
                results.append((moved, value, modes_of(value, edges)))
            for x, (moved, value, onward) in zip(spots, results):
                for c in range(3):
                    if final:
                        out_residual[c, x - REACH] = moved[c]
                    else:
                        if turn < 2:
                            step[c, x] = moved[c]
                        field[c, x] = value[c]
                if not final:
                    store_modes(x, onward)

        def update_body(trip, carry, low=low, update_layers=update_layers):
            update_layers([low + TOGETHER * trip + i for i in range(TOGETHER)])
            return carry

        trips = (high - low) // TOGETHER
        lax.fori_loop(0, trips, update_body, 0)
        if low + TOGETHER * trips < high:
            update_layers(list(range(low + TOGETHER * trips, high)))
        if turn == 2:
            for c in range(3):
                out_solution[c] = field[c, REACH : REACH + layers, :ROWS]


def vmem(count):
    return [pl.BlockSpec(memory_space=pltpu.VMEM)] * count


def tiles(*lead):
    return jax.ShapeDtypeStruct((*lead, ROWS, LANES), F32)


def solution(mesh):
    dims = tuple(mesh.shape[axis] for axis in AXES)

    def swap(value, axis, kind):
        return lax.ppermute(value, AXES, swap_pairs(dims, axis, kind))

    def body(forcing, guess, lame, shear):
        layers = lame.shape[0]
        wide = layers + 2 * REACH
        params = pltpu.CompilerParams(vmem_limit_bytes=32 * 1024 * 1024)
        given = (forcing, guess, lame, shear)
        *fields, own, z_near, z_far = pl.pallas_call(
            pack_first,
            out_shape=[jax.ShapeDtypeStruct(a.shape, F32) for a in given] + [tiles(layers)] + [tiles(layers // 4)] * 2,
            in_specs=[pl.BlockSpec(memory_space=pltpu.HBM)] * 4,
            out_specs=vmem(7),
            scratch_shapes=[pltpu.SemaphoreType.DMA((4,))],
            compiler_params=params,
            name="pack_first",
        )(*(pltpu.with_memory_space_constraint(a, pltpu.HBM) for a in given))
        y0_near, y0_far, x_near, x_far = pl.pallas_call(
            pack_rest,
            out_shape=[tiles(4 * layers)] * 2 + [tiles(X_TILES)] * 2,
            in_specs=vmem(4),
            out_specs=vmem(4),
            compiler_params=params,
            name="pack_rest",
        )(*fields)
        z_far = swap(z_far, 2, 1)
        z_near = swap(z_near, 2, 0)
        y0_near = swap(y0_near, 1, 0)
        y0_far = swap(y0_far, 1, 1)
        full, x_near, x_far = pl.pallas_call(
            pack_second,
            out_shape=[tiles(layers), tiles(X_TILES), tiles(X_TILES)],
            in_specs=vmem(5),
            out_specs=vmem(3),
            compiler_params=params,
            name="pack_second",
        )(own, z_near, z_far, x_near, x_far)
        x_near = swap(x_near, 0, 0)
        x_far = swap(x_far, 0, 1)
        y1_near, y1_far = pl.pallas_call(
            pack_third,
            out_shape=[tiles(X_TILES + layers // 2)] * 2,
            in_specs=vmem(3),
            out_specs=vmem(2),
            compiler_params=params,
            name="pack_third",
        )(full, x_near, x_far)
        y1_near = swap(y1_near, 1, 0)
        y1_far = swap(y1_far, 1, 1)
        block = (2 * ROWS, LANES)
        return pl.pallas_call(
            smooth,
            out_shape=[tiles(3, layers), tiles(3, layers)],
            in_specs=vmem(11),
            out_specs=vmem(2),
            scratch_shapes=[
                pltpu.VMEM((8, wide, *block), F32),
                pltpu.VMEM((wide, *block), F32),
                pltpu.VMEM((8, 3, *block), F32),
                pltpu.VMEM((6, 3, *block), F32),
                pltpu.VMEM((3, 3, *block), F32),
                pltpu.VMEM((3, 3, *block), F32),
                pltpu.VMEM((3, 3, *block), F32),
                pltpu.VMEM((6, wide, *block), F32),
                pltpu.VMEM((3, wide, *block), F32),
                pltpu.VMEM((wide, 12, *block), F32),
                pltpu.VMEM((wide, 12, *block), F32),
            ],
            compiler_params=params,
            name="smooth",
        )(*fields, full, y0_near, y0_far, x_near, x_far, y1_near, y1_far)

    in_specs = (P(None, *AXES), P(None, *AXES), P(*AXES), P(*AXES))
    out_specs = (P(None, *AXES), P(None, *AXES))
    return jax.shard_map(body, mesh=mesh, in_specs=in_specs, out_specs=out_specs, check_vma=False)
```

```python
import itertools

import jax
import jax.numpy as jnp
from jax import lax
from jax.experimental import pallas as pl
from jax.experimental.pallas import tpu as pltpu
from jax.sharding import PartitionSpec as P

AXES = ("gx", "gy", "gz")
REACH = 4
F32 = jnp.float32
LANES = 128
TOGETHER = 9
FIRST_TOGETHER = 12
INVERSE_TOGETHER = 11
FORCES_TOGETHER = 6
ROWS = 8


def swap_pairs(dims, axis, kind):
    other = (1, 0, 1)[axis]

    def place(spot):
        return (spot[0] * dims[1] + spot[1]) * dims[2] + spot[2]

    pairs = []
    for spot in itertools.product(*(range(size) for size in dims)):
        goal = list(spot)
        mate = (spot[axis] ^ 1) if kind == 0 else ((spot[axis] + 1) ^ 1) - 1
        if 0 <= mate < dims[axis]:
            goal[axis] = mate
        else:
            goal[other] ^= 1
        pairs.append((place(spot), place(goal)))
    return pairs


def iota(shape, dim):
    return lax.broadcasted_iota(jnp.int32, shape, dim)


def half_turn(tile):
    return pltpu.roll(tile, ROWS // 2, 0)


def even(axis):
    return lax.rem(lax.axis_index(axis), 2) == 0


def at_end(axis):
    place = lax.axis_index(axis)
    return jnp.logical_or(place == 0, place == lax.axis_size(axis) - 1)


def fields_of(forcing, guess, lame, shear):
    return [guess.at[c] for c in range(3)] + [forcing.at[c] for c in range(3)] + [lame, shear]


def row_mask(flag):
    low = iota((ROWS, LANES), 0) < ROWS // 2
    return jnp.logical_xor(low, jnp.broadcast_to(flag, low.shape))


X_LAYERS = (4, 4, 4, 3, 3, 3, 4, 4, 4)
X_STARTS = tuple(sum(X_LAYERS[:f]) for f in range(9))
X_TILES = sum(X_LAYERS)


def pack_first(forcing_hbm, guess_hbm, lame_hbm, shear_hbm, forcing, guess, lame, shear, own, z_near, z_far, arrived):
    pairs = ((forcing_hbm, forcing), (guess_hbm, guess), (lame_hbm, lame), (shear_hbm, shear))
    copies = [pltpu.make_async_copy(*pair, arrived.at[i]) for i, pair in enumerate(pairs)]
    for copy in copies:
        copy.start()
    for copy in copies:
        copy.wait()
    fields = fields_of(forcing, guess, lame, shear)
    layers = own.shape[0]
    slot = lax.rem(iota((ROWS, LANES), 1), 16)
    group = lax.div(iota((ROWS, LANES), 1), 16)
    quarter = lax.div(slot, 4)
    edges = []
    for x in range(layers):
        low = jnp.zeros((ROWS, LANES), F32)
        high = low
        for f in range(8):
            tile = fields[f][x]
            low = jnp.where(group == f, pltpu.roll(tile, (16 * f + 4) % LANES, 1), low)
            high = jnp.where(group == f, pltpu.roll(tile, (16 * f + 12) % LANES, 1), high)
        tile = jnp.where(slot < 8, low, high)
        own[x] = tile
        edges.append(tile)
    up_first = even("gz")
    quads = layers // 4
    for q in range(quads):
        up = edges[q]
        down = edges[q]
        for j in range(4):
            tile = edges[q + quads * j]
            up = jnp.where(quarter == j, pltpu.roll(tile, (4 * j - 8) % LANES, 1), up)
            down = jnp.where(quarter == j, pltpu.roll(tile, (4 * j - 4) % LANES, 1), down)
        z_near[q] = jnp.where(up_first, up, down)
        z_far[q] = jnp.where(up_first, down, up)


def pack_rest(forcing, guess, lame, shear, y_near, y_far, x_near, x_far):
    fields = fields_of(forcing, guess, lame, shear)
    layers = lame.shape[0]
    keep = row_mask(even("gy"))
    half = layers // 2
    for f in range(8):
        for x in range(half):
            here = fields[f][x]
            there = half_turn(fields[f][x + half])
            y_near[f * half + x] = jnp.where(keep, here, there)
            y_far[f * half + x] = jnp.where(keep, there, here)
    up_first = even("gx")
    for f in range(8):
        count = X_LAYERS[f]
        last = layers - count
        for x in range(count):
            x_near[X_STARTS[f] + x] = fields[f][jnp.where(up_first, last, 0) + x]
            x_far[X_STARTS[f] + x] = fields[f][jnp.where(up_first, 0, last) + x]


def pack_second(own, z_near, z_far, x_near_in, x_far_in, full, x_near, x_far):
    layers = own.shape[0]
    filled = pl.ds(0, X_STARTS[8])
    x_near[filled] = x_near_in[filled]
    x_far[filled] = x_far_in[filled]
    quads = layers // 4
    slot = lax.rem(iota((ROWS, LANES), 1), 16)
    forward = even("gz")
    ends = at_end("gz")
    for q in range(quads):
        near = z_near[q]
        far = jnp.where(ends, 0.0, z_far[q])
        behind = jnp.where(forward, far, near)
        ahead = jnp.where(forward, near, far)
        for j in range(4):
            x = q + quads * j
            tile = jnp.where(slot < 4, pltpu.roll(behind, (-4 * j) % LANES, 1), own[x])
            full[x] = jnp.where(slot >= 12, pltpu.roll(ahead, (12 - 4 * j) % LANES, 1), tile)
    up_first = even("gx")
    last = layers - 4
    for x in range(4):
        x_near[X_STARTS[8] + x] = full[jnp.where(up_first, last, 0) + x]
        x_far[X_STARTS[8] + x] = full[jnp.where(up_first, 0, last) + x]


def pack_third(full, x_near, x_far, y_near, y_far):
    keep = row_mask(even("gy"))
    half = full.shape[0] // 2
    for i in range(X_TILES):
        here = x_near[i]
        there = half_turn(x_far[i])
        y_near[i] = jnp.where(keep, here, there)
        y_far[i] = jnp.where(keep, there, here)
    for x in range(half):
        here = full[x]
        there = half_turn(full[x + half])
        y_near[X_TILES + x] = jnp.where(keep, here, there)
        y_far[X_TILES + x] = jnp.where(keep, there, here)


def turn_rows(tile, shift, seam):
    first = pltpu.roll(tile[:ROWS], shift, 0)
    second = pltpu.roll(tile[ROWS:], shift, 0)
    crossing = iota((ROWS, LANES), 0) == seam
    return jnp.concatenate([jnp.where(crossing, second, first), jnp.where(crossing, first, second)], 0)


def row_next(tile):
    return turn_rows(tile, ROWS - 1, ROWS - 1)


def row_prev(tile):
    return turn_rows(tile, 1, 0)


def lane_next(tile):
    return pltpu.roll(tile, LANES - 1, 1)


def lane_prev(tile):
    return pltpu.roll(tile, 1, 1)


def node_modes(here, beyond):
    total = here + beyond
    change = beyond - here
    total_y = row_next(total)
    change_y = row_next(change)
    return (total + total_y, total_y - total, change + change_y, change_y - change)


def element_modes(lower, upper, lam, mu):
    s = [[lower[c][m] + upper[c][m] for m in range(4)] for c in range(3)]
    d = [[upper[c][m] - lower[c][m] for m in range(4)] for c in range(3)]
    mu2 = mu + mu
    lam3 = lam * (1.0 / 3.0)
    mu3 = mu * (1.0 / 3.0)
    stiff = (lam3 + 4.0 * mu3) * (1.0 / 3.0)
    pressure = lam * (d[0][0] + s[1][1] + s[2][2])
    xx = pressure + mu2 * d[0][0]
    yy = pressure + mu2 * s[1][1]
    zz = pressure + mu2 * s[2][2]
    xy = mu * (s[0][1] + d[1][0])
    xz = mu * (s[0][2] + d[2][0])
    yz = mu * (s[1][2] + s[2][1])
    along_y = lam3 * (d[0][1] + s[2][3])
    along_z = lam3 * (d[0][2] + s[1][3])
    along_x = lam3 * (d[1][1] + d[2][2])
    twist = mu3 * (s[0][3] + d[1][2] + d[2][1])
    fs = [
        [None, xy, xz, twist + mu3 * s[0][3]],
        [None, yy, yz, along_z + mu * s[1][3]],
        [None, yz, zz, along_y + mu * s[2][3]],
    ]
    fd = [
        [xx, along_y + mu * d[0][1], along_z + mu * d[0][2], stiff * d[0][3]],
        [xy, along_x + mu * d[1][1], twist + mu3 * d[1][2], stiff * d[1][3]],
        [xz, twist + mu3 * d[2][1], along_x + mu * d[2][2], stiff * d[2][3]],
    ]
    low = [[-fd[c][0]] + [fs[c][m] - fd[c][m] for m in range(1, 4)] for c in range(3)]
    high = [[fd[c][0]] + [fs[c][m] + fd[c][m] for m in range(1, 4)] for c in range(3)]
    return low, high


def gather_rows(modes):
    total = (modes[0] - modes[1]) + row_prev(modes[0] + modes[1])
    change = (modes[2] - modes[3]) + row_prev(modes[2] + modes[3])
    return total - change, total + change


def apply_inverse(inv, vec):
    return (
        inv[0] * vec[0] + inv[1] * vec[1] + inv[2] * vec[2],
        inv[1] * vec[0] + inv[3] * vec[1] + inv[4] * vec[2],
        inv[2] * vec[0] + inv[4] * vec[1] + inv[5] * vec[2],
    )


def block_parts(lam, mu, shift):
    stiff = lam + 4.0 * mu
    cross = lam + mu
    stiff = stiff + shift[0](stiff)
    behind = shift[1](cross)
    total = behind + cross
    change = behind - cross
    total_y = row_prev(total)
    change_y = row_prev(change)
    return (stiff + row_prev(stiff), total_y - total, change_y + change, change_y - change)


def block_inverse(before, after, valid):
    diag = (16.0 / 9.0) * (before[0] + after[0])
    p = (4.0 / 3.0) * (before[1] - after[1])
    q = (4.0 / 3.0) * (before[2] - after[2])
    s = (4.0 / 3.0) * (before[3] + after[3])
    c00 = diag * diag - s * s
    c01 = q * s - p * diag
    c02 = p * s - q * diag
    scale = 1.0 / (diag * c00 + p * c01 + q * c02)
    cof = (c00, c01, c02, diag * diag - q * q, p * q - diag * s, diag * diag - p * p)
    return [jnp.where(valid, entry * scale, 0.0) for entry in cof]


def sweep(low, high, body, carry, together):
    whole = (high - low) // together

    def many(trip, carry):
        for i in range(together):
            carry = body(low + trip * together + i, carry)
        return carry

    carry = lax.fori_loop(0, whole, many, carry)
    for x in range(low + whole * together, high):
        carry = body(x, carry)
    return carry


def step_weights():
    low, high = (0.3, 3.0)
    theta = (high + low) / 2.0
    delta = (high - low) / 2.0
    sigma = theta / delta
    weights = [(0.0, 1.0 / theta)]
    rho_old = 1.0 / sigma
    for _ in range(2):
        rho = 1.0 / (2.0 * sigma - rho_old)
        weights.append((rho * rho_old, 2.0 * rho / delta))
        rho_old = rho
    return weights


def smooth(
    forcing, guess, lame, shear, full, y0_near, y0_far, x_near, x_far, y1_near, y1_far,
    solution_hbm, residual_hbm,
    out_solution, out_residual, left, field, edge, strip, strip_inv, strip_step, strip_push, joined, inv, step, modes, forces,
):
    own_fields = fields_of(forcing, guess, lame, shear)
    layers = full.shape[0]
    wide = layers + 2 * REACH
    half = layers // 2
    tall = 2 * ROWS

    y_keep = row_mask(jnp.logical_not(even("gy")))
    y_ends = at_end("gy")
    x_forward = even("gx")
    x_ends = at_end("gx")

    def scaled(f, tile):
        return tile * (1.0 / 16.0) if f in (6, 7) else tile

    def beside(near, far):
        far = jnp.where(y_ends, 0.0, far)
        return jnp.where(y_keep, near, far), half_turn(jnp.where(y_keep, far, near))

    def target(f):
        return field.at[f] if f < 8 else edge

    zero = jnp.zeros((tall, LANES), F32)
    for f in range(3, 6):
        field[f, 0] = zero
        field[f, wide - 1] = zero
    for f in range(9):
        for x in range(half):
            if f < 8:
                i = f * half + x
                first, second = beside(y0_near[i], y0_far[i])
                target(f)[REACH + x, :ROWS] = scaled(f, own_fields[f][x])
                target(f)[REACH + x + half, :ROWS] = scaled(f, own_fields[f][x + half])
            else:
                i = X_TILES + x
                first, second = beside(y1_near[i], y1_far[i])
                edge[REACH + x, :ROWS] = full[x]
                edge[REACH + x + half, :ROWS] = full[x + half]
            target(f)[REACH + x, ROWS:] = scaled(f, first)
            target(f)[REACH + x + half, ROWS:] = scaled(f, second)
    for f in range(9):
        count = X_LAYERS[f]
        ahead = REACH + layers
        behind = REACH - count
        to_near = jnp.where(x_forward, ahead, behind)
        to_far = jnp.where(x_forward, behind, ahead)
        for x in range(count):
            i = X_STARTS[f] + x
            target(f)[to_near + x, :ROWS] = scaled(f, x_near[i])
            target(f)[to_far + x, :ROWS] = jnp.where(x_ends, 0.0, scaled(f, x_far[i]))
            first, second = beside(y1_near[i], y1_far[i])
            target(f)[to_near + x, ROWS:] = scaled(f, first)
            target(f)[to_far + x, ROWS:] = jnp.where(x_ends, 0.0, scaled(f, second))

    lane = iota((tall, LANES), 1)
    row = iota((tall, LANES), 0)
    group = lax.div(lane, 16)
    slot = lax.rem(lane, 16)
    first_lane = lane == 0
    last_lane = lane == LANES - 1

    groups = wide // 3

    def choose(tiles):
        chosen = tiles[0]
        for g in range(1, groups):
            chosen = jnp.where(group == g, tiles[g], chosen)
        return chosen

    for i in range(3):
        rows_of = [edge[3 * g + i] for g in range(groups)]
        turned = [
            pltpu.roll(choose([rows_of[(f + d) % groups] for f in range(8)]), 16 * d, 1) if d else choose(rows_of)
            for d in range(groups)
        ]
        for f in range(8):
            strip[f, i] = scaled(f, choose([turned[(g - f) % groups] for g in range(groups)]))

    place_x, place_y, place_z = (lax.axis_index(axis) for axis in AXES)
    count_x, count_y, count_z = (lax.axis_size(axis) for axis in AXES)
    from_x = jnp.where(place_x == 0, REACH, 0)
    to_x = jnp.where(place_x == count_x - 1, REACH + layers, wide)
    row_from = jnp.where(place_y == count_y - 1, ROWS + 4, ROWS)
    row_to = jnp.where(place_y == 0, ROWS + 4, tall)
    row_ok = jnp.logical_or(row < ROWS, jnp.logical_and(row >= row_from, row < row_to))
    slot_from = jnp.where(place_z == 0, 4, 0)
    slot_to = jnp.where(place_z == count_z - 1, 12, 16)
    slot_ok = jnp.logical_and(row_ok, jnp.logical_and(slot >= slot_from, slot < slot_to))

    def strip_next(tiles):
        return [tiles[1], tiles[2], pltpu.roll(tiles[0], LANES - 16, 1)]

    def strip_prev(tiles):
        return [pltpu.roll(tiles[2], 16, 1), tiles[0], tiles[1]]

    def at_high(tile, g):
        return pltpu.roll(tile, lax.rem(LANES + 115 - 16 * g, LANES), 1)

    def at_low(tile, g):
        return pltpu.roll(tile, lax.rem(LANES + 125 - 16 * g, LANES), 1)

    parts = [block_parts(strip[6, i], strip[7, i], (lane_prev, lane_prev)) for i in range(3)]
    previous = [strip_prev([parts[i][k] for i in range(3)]) for k in range(4)]
    for i in range(3):
        layer = 3 * group + i
        valid = jnp.logical_and(slot_ok, jnp.logical_and(layer >= from_x, layer < to_x))
        entries = block_inverse([previous[k][i] for k in range(4)], parts[i], valid)
        for k in range(6):
            strip_inv[k, i] = entries[k]

    def main_parts(x):
        g = lax.div(x, 3)
        i = lax.rem(x, 3)
        lam_low = at_low(strip[6, i], g)
        mu_low = at_low(strip[7, i], g)

        def shift_stiff(tile):
            return jnp.where(first_lane, lam_low + 4.0 * mu_low, lane_prev(tile))

        def shift_cross(tile):
            return jnp.where(first_lane, lam_low + mu_low, lane_prev(tile))

        return block_parts(field[6, x], field[7, x], (shift_stiff, shift_cross))

    def inverse_body(x, before):
        after = main_parts(x)
        valid = jnp.logical_and(row_ok, jnp.logical_and(x >= from_x, x < to_x))
        entries = block_inverse(before, after, valid)
        for k in range(6):
            inv[k, x] = entries[k]
        return after

    sweep(1, wide - 1, inverse_body, main_parts(0), INVERSE_TOGETHER)

    def place_of(x):
        return lax.div(x, 3), lax.rem(x, 3)

    def modes_of(tiles, edges):
        beyond = [
            jnp.where(last_lane, edges[0], lane_next(tiles[0])),
            lane_next(jnp.where(first_lane, edges[0], tiles[1])),
            jnp.where(last_lane, edges[1], lane_next(tiles[2])),
        ]
        return [node_modes(tiles[c], beyond[c]) for c in range(3)]

    def pushed_along(tiles, edges):
        return [
            jnp.where(first_lane, edges[1], lane_prev(tiles[0])),
            lane_prev(jnp.where(last_lane, edges[2], tiles[1])),
            jnp.where(first_lane, edges[2], lane_prev(tiles[2])),
        ]

    def join_edges(push):
        for i in range(3):
            joined[0, i] = jnp.where(slot == 13, pltpu.roll(strip[1, i], 1, 1), strip[0, i])
            if push:
                joined[1, i] = jnp.where(slot == 13, pltpu.roll(strip_push[0, i], 10, 1), strip[2, i])
                last = pltpu.roll(strip_push[2, i], 10, 1)
                joined[2, i] = jnp.where(slot == 13, last, pltpu.roll(strip_push[1, i], 9, 1))
            else:
                joined[1, i] = strip[2, i]

    def edges_of(x, which):
        g, i = place_of(x)
        return [at_high(joined[k, i], g) if k in which else None for k in range(3)]

    join_edges(False)

    def store_modes(x, values):
        for c in range(3):
            for m in range(4):
                modes[x, 4 * c + m] = values[c][m]

    def first_modes(trip, carry):
        spots = [FIRST_TOGETHER * trip + i for i in range(FIRST_TOGETHER)]
        loaded = [([field[c, x] for c in range(3)], edges_of(x, (0, 1))) for x in spots]
        values = [modes_of(*pair) for pair in loaded]
        for x, value in zip(spots, values):
            store_modes(x, value)
        return carry

    lax.fori_loop(0, wide // FIRST_TOGETHER, first_modes, 0)

    copies = []
    weights = step_weights()
    for turn in range(4):
        final = turn == 3
        here = [[strip[c, i] for i in range(3)] for c in range(3)]
        node = [[node_modes(here[c][i], lane_next(here[c][i])) for c in range(3)] for i in range(3)]
        above = [[[None] * 4 for c in range(3)] for i in range(3)]
        for c in range(3):
            for m in range(4):
                moved = strip_next([node[i][c][m] for i in range(3)])
                for i in range(3):
                    above[i][c][m] = moved[i]
        push = [element_modes(node[i], above[i], strip[6, i], strip[7, i]) for i in range(3)]
        pull = [[None] * 3 for i in range(3)]
        for c in range(3):
            total = [[None] * 4 for i in range(3)]
            for m in range(4):
                moved = strip_prev([push[i][1][c][m] for i in range(3)])
                for i in range(3):
                    total[i][m] = moved[i] + push[i][0][c][m]
            for i in range(3):
                stay, go = gather_rows(total[i])
                strip_push[c, i] = go
                pull[i][c] = stay + lane_prev(go)

        low, high = 1 + turn, wide - 1 - turn

        if not final:
            keep, add = weights[turn]
            for i in range(3):
                rest = [strip[3 + c, i] - pull[i][c] for c in range(3)]
                moved = apply_inverse([strip_inv[k, i] for k in range(6)], rest)
                for c in range(3):
                    change = add * moved[c]
                    if turn > 0:
                        change = keep * strip_step[c, i] + change
                    strip_step[c, i] = change
                    strip[c, i] = strip[c, i] + change

        join_edges(True)

        for part in range(2):
            rows = pl.ds(part * ROWS, ROWS)

            def load_modes(x, rows=rows):
                return [[modes[x, 4 * c + m, rows] for m in range(4)] for c in range(3)]

            def forces_body(x, carry, rows=rows, load_modes=load_modes):
                lower, pushed = carry
                upper = load_modes(x + 1)
                down, up = element_modes(lower, upper, field[6, x, rows], field[7, x, rows])
                for c in range(3):
                    for m in range(4):
                        forces[x, 4 * c + m, rows] = pushed[c][m] + down[c][m]
                return upper, up

            nothing = [[jnp.zeros((ROWS, LANES), F32) for m in range(4)] for c in range(3)]
            sweep(low - 1, high, forces_body, (load_modes(low - 1), nothing), FORCES_TOGETHER)

        def update_layers(spots, turn=turn, final=final):
            loaded = []
            for x in spots:
                loaded.append(
                    (
                        [[forces[x, 4 * c + m] for m in range(4)] for c in range(3)],
                        edges_of(x, (1, 2) if final else (0, 1, 2)),
                        [field[3 + c, x] for c in range(3)],
                        [inv[k, x] for k in range(6)],
                        None if final else [field[c, x] for c in range(3)],
                        [step[c, x] for c in range(3)] if 0 < turn < 3 else None,
                    )
                )
            results = []
            for force, edges, load, block, value, before in loaded:
                gathered = [gather_rows(force[c]) for c in range(3)]
                come = pushed_along([go for stay, go in gathered], edges)
                rest = [load[c] - (gathered[c][0] + come[c]) for c in range(3)]
                if final:
                    moved = apply_inverse([entry[:ROWS] for entry in block], [part[:ROWS] for part in rest])
                    results.append((moved, None, None))
                    continue
                keep, add = weights[turn]
                moved = [add * part for part in apply_inverse(block, rest)]
                if turn > 0:
                    moved = [keep * before[c] + moved[c] for c in range(3)]
                value = [value[c] + moved[c] for c in range(3)]
                results.append((moved, value, modes_of(value, edges)))
            for x, (moved, value, onward) in zip(spots, results):
                for c in range(3):
                    if final:
                        out_residual[c, x - REACH] = moved[c]
                    else:
                        if turn < 2:
                            step[c, x] = moved[c]
                        field[c, x] = value[c]
                if not final:
                    store_modes(x, onward)

        def update_body(trip, carry, low=low, update_layers=update_layers):
            update_layers([low + TOGETHER * trip + i for i in range(TOGETHER)])
            return carry

        trips = (high - low) // TOGETHER
        lax.fori_loop(0, trips, update_body, 0)
        if final:
            done = pl.ds(0, TOGETHER * trips)
            copies.append(pltpu.make_async_copy(out_residual.at[:, done], residual_hbm.at[:, done], left.at[1]))
            copies[-1].start()
        if low + TOGETHER * trips < high:
            update_layers(list(range(low + TOGETHER * trips, high)))
        if final and TOGETHER * trips < layers:
            rest = pl.ds(TOGETHER * trips, layers - TOGETHER * trips)
            copies.append(pltpu.make_async_copy(out_residual.at[:, rest], residual_hbm.at[:, rest], left.at[2]))
            copies[-1].start()
        if turn == 2:
            for c in range(3):
                out_solution[c] = field[c, REACH : REACH + layers, :ROWS]
            copies.append(pltpu.make_async_copy(out_solution, solution_hbm, left.at[0]))
            copies[-1].start()
    for copy in copies:
        copy.wait()


def vmem(count):
    return [pl.BlockSpec(memory_space=pltpu.VMEM)] * count


def tiles(*lead):
    return jax.ShapeDtypeStruct((*lead, ROWS, LANES), F32)


def solution(mesh):
    dims = tuple(mesh.shape[axis] for axis in AXES)

    def swap(value, axis, kind):
        return lax.ppermute(value, AXES, swap_pairs(dims, axis, kind))

    def body(forcing, guess, lame, shear):
        layers = lame.shape[0]
        wide = layers + 2 * REACH
        params = pltpu.CompilerParams(vmem_limit_bytes=32 * 1024 * 1024)
        given = (forcing, guess, lame, shear)
        *fields, own, z_near, z_far = pl.pallas_call(
            pack_first,
            out_shape=[jax.ShapeDtypeStruct(a.shape, F32) for a in given] + [tiles(layers)] + [tiles(layers // 4)] * 2,
            in_specs=[pl.BlockSpec(memory_space=pltpu.HBM)] * 4,
            out_specs=vmem(7),
            scratch_shapes=[pltpu.SemaphoreType.DMA((4,))],
            compiler_params=params,
            name="pack_first",
        )(*(pltpu.with_memory_space_constraint(a, pltpu.HBM) for a in given))
        y0_near, y0_far, x_near, x_far = pl.pallas_call(
            pack_rest,
            out_shape=[tiles(4 * layers)] * 2 + [tiles(X_TILES)] * 2,
            in_specs=vmem(4),
            out_specs=vmem(4),
            compiler_params=params,
            name="pack_rest",
        )(*fields)
        z_far = swap(z_far, 2, 1)
        z_near = swap(z_near, 2, 0)
        y0_near = swap(y0_near, 1, 0)
        y0_far = swap(y0_far, 1, 1)
        full, x_near, x_far = pl.pallas_call(
            pack_second,
            out_shape=[tiles(layers), tiles(X_TILES), tiles(X_TILES)],
            in_specs=vmem(5),
            out_specs=vmem(3),
            compiler_params=params,
            name="pack_second",
        )(own, z_near, z_far, x_near, x_far)
        x_near = swap(x_near, 0, 0)
        x_far = swap(x_far, 0, 1)
        y1_near, y1_far = pl.pallas_call(
            pack_third,
            out_shape=[tiles(X_TILES + layers // 2)] * 2,
            in_specs=vmem(3),
            out_specs=vmem(2),
            compiler_params=params,
            name="pack_third",
        )(full, x_near, x_far)
        y1_near = swap(y1_near, 1, 0)
        y1_far = swap(y1_far, 1, 1)
        block = (2 * ROWS, LANES)
        return pl.pallas_call(
            smooth,
            out_shape=[tiles(3, layers), tiles(3, layers)],
            in_specs=vmem(11),
            out_specs=[pl.BlockSpec(memory_space=pltpu.HBM)] * 2,
            scratch_shapes=[
                pltpu.VMEM((3, layers, ROWS, LANES), F32),
                pltpu.VMEM((3, layers, ROWS, LANES), F32),
                pltpu.SemaphoreType.DMA((3,)),
                pltpu.VMEM((8, wide, *block), F32),
                pltpu.VMEM((wide, *block), F32),
                pltpu.VMEM((8, 3, *block), F32),
                pltpu.VMEM((6, 3, *block), F32),
                pltpu.VMEM((3, 3, *block), F32),
                pltpu.VMEM((3, 3, *block), F32),
                pltpu.VMEM((3, 3, *block), F32),
                pltpu.VMEM((6, wide, *block), F32),
                pltpu.VMEM((3, wide, *block), F32),
                pltpu.VMEM((wide, 12, *block), F32),
                pltpu.VMEM((wide, 12, *block), F32),
            ],
            compiler_params=params,
            name="smooth",
        )(*fields, full, y0_near, y0_far, x_near, x_far, y1_near, y1_far)

    in_specs = (P(None, *AXES), P(None, *AXES), P(*AXES), P(*AXES))
    out_specs = (P(None, *AXES), P(None, *AXES))
    return jax.shard_map(body, mesh=mesh, in_specs=in_specs, out_specs=out_specs, check_vma=False)
```

```python
import itertools

import jax
import jax.numpy as jnp
from jax import lax
from jax.experimental import pallas as pl
from jax.experimental.pallas import tpu as pltpu
from jax.sharding import PartitionSpec as P

AXES = ("gx", "gy", "gz")
REACH = 4
F32 = jnp.float32
LANES = 128
TOGETHER = 9
FIRST_TOGETHER = 24
INVERSE_TOGETHER = 22
FORCES_TOGETHER = 12
ROWS = 8


def swap_pairs(dims, axis, kind):
    other = (1, 0, 1)[axis]

    def place(spot):
        return (spot[0] * dims[1] + spot[1]) * dims[2] + spot[2]

    pairs = []
    for spot in itertools.product(*(range(size) for size in dims)):
        goal = list(spot)
        mate = (spot[axis] ^ 1) if kind == 0 else ((spot[axis] + 1) ^ 1) - 1
        if 0 <= mate < dims[axis]:
            goal[axis] = mate
        else:
            goal[other] ^= 1
        pairs.append((place(spot), place(goal)))
    return pairs


def iota(shape, dim):
    return lax.broadcasted_iota(jnp.int32, shape, dim)


def half_turn(tile):
    return pltpu.roll(tile, ROWS // 2, 0)


def even(axis):
    return lax.rem(lax.axis_index(axis), 2) == 0


def at_end(axis):
    place = lax.axis_index(axis)
    return jnp.logical_or(place == 0, place == lax.axis_size(axis) - 1)


def fields_of(forcing, guess, lame, shear):
    return [guess.at[c] for c in range(3)] + [forcing.at[c] for c in range(3)] + [lame, shear]


def row_mask(flag):
    low = iota((ROWS, LANES), 0) < ROWS // 2
    return jnp.logical_xor(low, jnp.broadcast_to(flag, low.shape))


X_LAYERS = (4, 4, 4, 3, 3, 3, 4, 4, 4)
X_STARTS = tuple(sum(X_LAYERS[:f]) for f in range(9))
X_TILES = sum(X_LAYERS)


def pack_first(forcing_hbm, guess_hbm, lame_hbm, shear_hbm, forcing, guess, lame, shear, own, z_near, z_far, arrived):
    pairs = ((forcing_hbm, forcing), (guess_hbm, guess), (lame_hbm, lame), (shear_hbm, shear))
    copies = [pltpu.make_async_copy(*pair, arrived.at[i]) for i, pair in enumerate(pairs)]
    for copy in copies:
        copy.start()
    for copy in copies:
        copy.wait()
    fields = fields_of(forcing, guess, lame, shear)
    layers = own.shape[0]
    slot = lax.rem(iota((ROWS, LANES), 1), 16)
    group = lax.div(iota((ROWS, LANES), 1), 16)
    quarter = lax.div(slot, 4)
    edges = []
    for x in range(layers):
        low = jnp.zeros((ROWS, LANES), F32)
        high = low
        for f in range(8):
            tile = fields[f][x]
            low = jnp.where(group == f, pltpu.roll(tile, (16 * f + 4) % LANES, 1), low)
            high = jnp.where(group == f, pltpu.roll(tile, (16 * f + 12) % LANES, 1), high)
        tile = jnp.where(slot < 8, low, high)
        own[x] = tile
        edges.append(tile)
    up_first = even("gz")
    quads = layers // 4
    for q in range(quads):
        up = edges[q]
        down = edges[q]
        for j in range(4):
            tile = edges[q + quads * j]
            up = jnp.where(quarter == j, pltpu.roll(tile, (4 * j - 8) % LANES, 1), up)
            down = jnp.where(quarter == j, pltpu.roll(tile, (4 * j - 4) % LANES, 1), down)
        z_near[q] = jnp.where(up_first, up, down)
        z_far[q] = jnp.where(up_first, down, up)


def pack_rest(forcing, guess, lame, shear, y_near, y_far, x_near, x_far):
    fields = fields_of(forcing, guess, lame, shear)
    layers = lame.shape[0]
    keep = row_mask(even("gy"))
    half = layers // 2
    for f in range(8):
        for x in range(half):
            here = fields[f][x]
            there = half_turn(fields[f][x + half])
            y_near[f * half + x] = jnp.where(keep, here, there)
            y_far[f * half + x] = jnp.where(keep, there, here)
    up_first = even("gx")
    for f in range(8):
        count = X_LAYERS[f]
        last = layers - count
        for x in range(count):
            x_near[X_STARTS[f] + x] = fields[f][jnp.where(up_first, last, 0) + x]
            x_far[X_STARTS[f] + x] = fields[f][jnp.where(up_first, 0, last) + x]


def pack_second(own, z_near, z_far, x_near_in, x_far_in, full, x_near, x_far):
    layers = own.shape[0]
    filled = pl.ds(0, X_STARTS[8])
    x_near[filled] = x_near_in[filled]
    x_far[filled] = x_far_in[filled]
    quads = layers // 4
    slot = lax.rem(iota((ROWS, LANES), 1), 16)
    forward = even("gz")
    ends = at_end("gz")
    for q in range(quads):
        near = z_near[q]
        far = jnp.where(ends, 0.0, z_far[q])
        behind = jnp.where(forward, far, near)
        ahead = jnp.where(forward, near, far)
        for j in range(4):
            x = q + quads * j
            tile = jnp.where(slot < 4, pltpu.roll(behind, (-4 * j) % LANES, 1), own[x])
            full[x] = jnp.where(slot >= 12, pltpu.roll(ahead, (12 - 4 * j) % LANES, 1), tile)
    up_first = even("gx")
    last = layers - 4
    for x in range(4):
        x_near[X_STARTS[8] + x] = full[jnp.where(up_first, last, 0) + x]
        x_far[X_STARTS[8] + x] = full[jnp.where(up_first, 0, last) + x]


def pack_third(full, x_near, x_far, y_near, y_far):
    keep = row_mask(even("gy"))
    half = full.shape[0] // 2
    for i in range(X_TILES):
        here = x_near[i]
        there = half_turn(x_far[i])
        y_near[i] = jnp.where(keep, here, there)
        y_far[i] = jnp.where(keep, there, here)
    for x in range(half):
        here = full[x]
        there = half_turn(full[x + half])
        y_near[X_TILES + x] = jnp.where(keep, here, there)
        y_far[X_TILES + x] = jnp.where(keep, there, here)


def turn_rows(tile, shift, seam):
    first = pltpu.roll(tile[:ROWS], shift, 0)
    second = pltpu.roll(tile[ROWS:], shift, 0)
    crossing = iota((ROWS, LANES), 0) == seam
    return jnp.concatenate([jnp.where(crossing, second, first), jnp.where(crossing, first, second)], 0)


def row_next(tile):
    return turn_rows(tile, ROWS - 1, ROWS - 1)


def row_prev(tile):
    return turn_rows(tile, 1, 0)


def lane_next(tile):
    return pltpu.roll(tile, LANES - 1, 1)


def lane_prev(tile):
    return pltpu.roll(tile, 1, 1)


def node_modes(here, beyond):
    total = here + beyond
    change = beyond - here
    total_y = row_next(total)
    change_y = row_next(change)
    return (total + total_y, total_y - total, change + change_y, change_y - change)


def element_modes(lower, upper, lam, mu):
    s = [[lower[c][m] + upper[c][m] for m in range(4)] for c in range(3)]
    d = [[upper[c][m] - lower[c][m] for m in range(4)] for c in range(3)]
    mu2 = mu + mu
    lam3 = lam * (1.0 / 3.0)
    mu3 = mu * (1.0 / 3.0)
    stiff = (lam3 + 4.0 * mu3) * (1.0 / 3.0)
    pressure = lam * (d[0][0] + s[1][1] + s[2][2])
    xx = pressure + mu2 * d[0][0]
    yy = pressure + mu2 * s[1][1]
    zz = pressure + mu2 * s[2][2]
    xy = mu * (s[0][1] + d[1][0])
    xz = mu * (s[0][2] + d[2][0])
    yz = mu * (s[1][2] + s[2][1])
    along_y = lam3 * (d[0][1] + s[2][3])
    along_z = lam3 * (d[0][2] + s[1][3])
    along_x = lam3 * (d[1][1] + d[2][2])
    twist = mu3 * (s[0][3] + d[1][2] + d[2][1])
    fs = [
        [None, xy, xz, twist + mu3 * s[0][3]],
        [None, yy, yz, along_z + mu * s[1][3]],
        [None, yz, zz, along_y + mu * s[2][3]],
    ]
    fd = [
        [xx, along_y + mu * d[0][1], along_z + mu * d[0][2], stiff * d[0][3]],
        [xy, along_x + mu * d[1][1], twist + mu3 * d[1][2], stiff * d[1][3]],
        [xz, twist + mu3 * d[2][1], along_x + mu * d[2][2], stiff * d[2][3]],
    ]
    low = [[-fd[c][0]] + [fs[c][m] - fd[c][m] for m in range(1, 4)] for c in range(3)]
    high = [[fd[c][0]] + [fs[c][m] + fd[c][m] for m in range(1, 4)] for c in range(3)]
    return low, high


def gather_rows(modes):
    total = (modes[0] - modes[1]) + row_prev(modes[0] + modes[1])
    change = (modes[2] - modes[3]) + row_prev(modes[2] + modes[3])
    return total - change, total + change


def apply_inverse(inv, vec):
    return (
        inv[0] * vec[0] + inv[1] * vec[1] + inv[2] * vec[2],
        inv[1] * vec[0] + inv[3] * vec[1] + inv[4] * vec[2],
        inv[2] * vec[0] + inv[4] * vec[1] + inv[5] * vec[2],
    )


def block_parts(lam, mu, shift):
    stiff = lam + 4.0 * mu
    cross = lam + mu
    stiff = stiff + shift[0](stiff)
    behind = shift[1](cross)
    total = behind + cross
    change = behind - cross
    total_y = row_prev(total)
    change_y = row_prev(change)
    return (stiff + row_prev(stiff), total_y - total, change_y + change, change_y - change)


def block_inverse(before, after, valid):
    diag = (16.0 / 9.0) * (before[0] + after[0])
    p = (4.0 / 3.0) * (before[1] - after[1])
    q = (4.0 / 3.0) * (before[2] - after[2])
    s = (4.0 / 3.0) * (before[3] + after[3])
    c00 = diag * diag - s * s
    c01 = q * s - p * diag
    c02 = p * s - q * diag
    scale = 1.0 / (diag * c00 + p * c01 + q * c02)
    cof = (c00, c01, c02, diag * diag - q * q, p * q - diag * s, diag * diag - p * p)
    return [jnp.where(valid, entry * scale, 0.0) for entry in cof]


def sweep(low, high, body, carry, together):
    whole = (high - low) // together

    def many(trip, carry):
        for i in range(together):
            carry = body(low + trip * together + i, carry)
        return carry

    carry = lax.fori_loop(0, whole, many, carry)
    for x in range(low + whole * together, high):
        carry = body(x, carry)
    return carry


def step_weights():
    low, high = (0.3, 3.0)
    theta = (high + low) / 2.0
    delta = (high - low) / 2.0
    sigma = theta / delta
    weights = [(0.0, 1.0 / theta)]
    rho_old = 1.0 / sigma
    for _ in range(2):
        rho = 1.0 / (2.0 * sigma - rho_old)
        weights.append((rho * rho_old, 2.0 * rho / delta))
        rho_old = rho
    return weights


def smooth(
    forcing, guess, lame, shear, full, y0_near, y0_far, x_near, x_far, y1_near, y1_far,
    solution_hbm, residual_hbm,
    out_solution, out_residual, left, field, edge, strip, strip_inv, strip_step, strip_push, joined, inv, step, modes, forces,
):
    own_fields = fields_of(forcing, guess, lame, shear)
    layers = full.shape[0]
    wide = layers + 2 * REACH
    half = layers // 2
    tall = 2 * ROWS

    y_keep = row_mask(jnp.logical_not(even("gy")))
    y_ends = at_end("gy")
    x_forward = even("gx")
    x_ends = at_end("gx")

    def scaled(f, tile):
        return tile * (1.0 / 16.0) if f in (6, 7) else tile

    def beside(near, far):
        far = jnp.where(y_ends, 0.0, far)
        return jnp.where(y_keep, near, far), half_turn(jnp.where(y_keep, far, near))

    def target(f):
        return field.at[f] if f < 8 else edge

    zero = jnp.zeros((tall, LANES), F32)
    for f in range(3, 6):
        field[f, 0] = zero
        field[f, wide - 1] = zero
    for f in range(9):
        for x in range(half):
            if f < 8:
                i = f * half + x
                first, second = beside(y0_near[i], y0_far[i])
                target(f)[REACH + x, :ROWS] = scaled(f, own_fields[f][x])
                target(f)[REACH + x + half, :ROWS] = scaled(f, own_fields[f][x + half])
            else:
                i = X_TILES + x
                first, second = beside(y1_near[i], y1_far[i])
                edge[REACH + x, :ROWS] = full[x]
                edge[REACH + x + half, :ROWS] = full[x + half]
            target(f)[REACH + x, ROWS:] = scaled(f, first)
            target(f)[REACH + x + half, ROWS:] = scaled(f, second)
    for f in range(9):
        count = X_LAYERS[f]
        ahead = REACH + layers
        behind = REACH - count
        to_near = jnp.where(x_forward, ahead, behind)
        to_far = jnp.where(x_forward, behind, ahead)
        for x in range(count):
            i = X_STARTS[f] + x
            target(f)[to_near + x, :ROWS] = scaled(f, x_near[i])
            target(f)[to_far + x, :ROWS] = jnp.where(x_ends, 0.0, scaled(f, x_far[i]))
            first, second = beside(y1_near[i], y1_far[i])
            target(f)[to_near + x, ROWS:] = scaled(f, first)
            target(f)[to_far + x, ROWS:] = jnp.where(x_ends, 0.0, scaled(f, second))

    lane = iota((tall, LANES), 1)
    row = iota((tall, LANES), 0)
    group = lax.div(lane, 16)
    slot = lax.rem(lane, 16)
    first_lane = lane == 0
    last_lane = lane == LANES - 1

    groups = wide // 3

    def choose(tiles):
        chosen = tiles[0]
        for g in range(1, groups):
            chosen = jnp.where(group == g, tiles[g], chosen)
        return chosen

    for i in range(3):
        rows_of = [edge[3 * g + i] for g in range(groups)]
        turned = [
            pltpu.roll(choose([rows_of[(f + d) % groups] for f in range(8)]), 16 * d, 1) if d else choose(rows_of)
            for d in range(groups)
        ]
        for f in range(8):
            strip[f, i] = scaled(f, choose([turned[(g - f) % groups] for g in range(groups)]))

    place_x, place_y, place_z = (lax.axis_index(axis) for axis in AXES)
    count_x, count_y, count_z = (lax.axis_size(axis) for axis in AXES)
    from_x = jnp.where(place_x == 0, REACH, 0)
    to_x = jnp.where(place_x == count_x - 1, REACH + layers, wide)
    row_from = jnp.where(place_y == count_y - 1, ROWS + 4, ROWS)
    row_to = jnp.where(place_y == 0, ROWS + 4, tall)
    row_ok = jnp.logical_or(row < ROWS, jnp.logical_and(row >= row_from, row < row_to))
    slot_from = jnp.where(place_z == 0, 4, 0)
    slot_to = jnp.where(place_z == count_z - 1, 12, 16)
    slot_ok = jnp.logical_and(row_ok, jnp.logical_and(slot >= slot_from, slot < slot_to))

    def strip_next(tiles):
        return [tiles[1], tiles[2], pltpu.roll(tiles[0], LANES - 16, 1)]

    def strip_prev(tiles):
        return [pltpu.roll(tiles[2], 16, 1), tiles[0], tiles[1]]

    def at_high(tile, g):
        return pltpu.roll(tile, lax.rem(LANES + 115 - 16 * g, LANES), 1)

    def at_low(tile, g):
        return pltpu.roll(tile, lax.rem(LANES + 125 - 16 * g, LANES), 1)

    parts = [block_parts(strip[6, i], strip[7, i], (lane_prev, lane_prev)) for i in range(3)]
    previous = [strip_prev([parts[i][k] for i in range(3)]) for k in range(4)]
    for i in range(3):
        layer = 3 * group + i
        valid = jnp.logical_and(slot_ok, jnp.logical_and(layer >= from_x, layer < to_x))
        entries = block_inverse([previous[k][i] for k in range(4)], parts[i], valid)
        for k in range(6):
            strip_inv[k, i] = entries[k]

    def main_parts(x):
        g = lax.div(x, 3)
        i = lax.rem(x, 3)
        lam_low = at_low(strip[6, i], g)
        mu_low = at_low(strip[7, i], g)

        def shift_stiff(tile):
            return jnp.where(first_lane, lam_low + 4.0 * mu_low, lane_prev(tile))

        def shift_cross(tile):
            return jnp.where(first_lane, lam_low + mu_low, lane_prev(tile))

        return block_parts(field[6, x], field[7, x], (shift_stiff, shift_cross))

    def inverse_body(x, before):
        after = main_parts(x)
        valid = jnp.logical_and(row_ok, jnp.logical_and(x >= from_x, x < to_x))
        entries = block_inverse(before, after, valid)
        for k in range(6):
            inv[k, x] = entries[k]
        return after

    sweep(1, wide - 1, inverse_body, main_parts(0), INVERSE_TOGETHER)

    def place_of(x):
        return lax.div(x, 3), lax.rem(x, 3)

    def modes_of(tiles, edges):
        beyond = [
            jnp.where(last_lane, edges[0], lane_next(tiles[0])),
            lane_next(jnp.where(first_lane, edges[0], tiles[1])),
            jnp.where(last_lane, edges[1], lane_next(tiles[2])),
        ]
        return [node_modes(tiles[c], beyond[c]) for c in range(3)]

    def pushed_along(tiles, edges):
        return [
            jnp.where(first_lane, edges[1], lane_prev(tiles[0])),
            lane_prev(jnp.where(last_lane, edges[2], tiles[1])),
            jnp.where(first_lane, edges[2], lane_prev(tiles[2])),
        ]

    def join_edges(push):
        for i in range(3):
            joined[0, i] = jnp.where(slot == 13, pltpu.roll(strip[1, i], 1, 1), strip[0, i])
            if push:
                joined[1, i] = jnp.where(slot == 13, pltpu.roll(strip_push[0, i], 10, 1), strip[2, i])
                last = pltpu.roll(strip_push[2, i], 10, 1)
                joined[2, i] = jnp.where(slot == 13, last, pltpu.roll(strip_push[1, i], 9, 1))
            else:
                joined[1, i] = strip[2, i]

    def edges_of(x, which):
        g, i = place_of(x)
        return [at_high(joined[k, i], g) if k in which else None for k in range(3)]

    join_edges(False)

    def store_modes(x, values):
        for c in range(3):
            for m in range(4):
                modes[x, 4 * c + m] = values[c][m]

    def first_modes(trip, carry):
        spots = [FIRST_TOGETHER * trip + i for i in range(FIRST_TOGETHER)]
        loaded = [([field[c, x] for c in range(3)], edges_of(x, (0, 1))) for x in spots]
        values = [modes_of(*pair) for pair in loaded]
        for x, value in zip(spots, values):
            store_modes(x, value)
        return carry

    lax.fori_loop(0, wide // FIRST_TOGETHER, first_modes, 0)

    copies = []
    weights = step_weights()
    for turn in range(4):
        final = turn == 3
        here = [[strip[c, i] for i in range(3)] for c in range(3)]
        node = [[node_modes(here[c][i], lane_next(here[c][i])) for c in range(3)] for i in range(3)]
        above = [[[None] * 4 for c in range(3)] for i in range(3)]
        for c in range(3):
            for m in range(4):
                moved = strip_next([node[i][c][m] for i in range(3)])
                for i in range(3):
                    above[i][c][m] = moved[i]
        push = [element_modes(node[i], above[i], strip[6, i], strip[7, i]) for i in range(3)]
        pull = [[None] * 3 for i in range(3)]
        for c in range(3):
            total = [[None] * 4 for i in range(3)]
            for m in range(4):
                moved = strip_prev([push[i][1][c][m] for i in range(3)])
                for i in range(3):
                    total[i][m] = moved[i] + push[i][0][c][m]
            for i in range(3):
                stay, go = gather_rows(total[i])
                strip_push[c, i] = go
                pull[i][c] = stay + lane_prev(go)

        low, high = 1 + turn, wide - 1 - turn

        if not final:
            keep, add = weights[turn]
            for i in range(3):
                rest = [strip[3 + c, i] - pull[i][c] for c in range(3)]
                moved = apply_inverse([strip_inv[k, i] for k in range(6)], rest)
                for c in range(3):
                    change = add * moved[c]
                    if turn > 0:
                        change = keep * strip_step[c, i] + change
                    strip_step[c, i] = change
                    strip[c, i] = strip[c, i] + change

        join_edges(True)

        for part in range(2):
            rows = pl.ds(part * ROWS, ROWS)

            def load_modes(x, rows=rows):
                return [[modes[x, 4 * c + m, rows] for m in range(4)] for c in range(3)]

            def forces_body(x, carry, rows=rows, load_modes=load_modes):
                lower, pushed = carry
                upper = load_modes(x + 1)
                down, up = element_modes(lower, upper, field[6, x, rows], field[7, x, rows])
                for c in range(3):
                    for m in range(4):
                        forces[x, 4 * c + m, rows] = pushed[c][m] + down[c][m]
                return upper, up

            nothing = [[jnp.zeros((ROWS, LANES), F32) for m in range(4)] for c in range(3)]
            sweep(low - 1, high, forces_body, (load_modes(low - 1), nothing), FORCES_TOGETHER)

        def update_layers(spots, turn=turn, final=final):
            loaded = []
            for x in spots:
                loaded.append(
                    (
                        [[forces[x, 4 * c + m] for m in range(4)] for c in range(3)],
                        edges_of(x, (1, 2) if final else (0, 1, 2)),
                        [field[3 + c, x] for c in range(3)],
                        [inv[k, x] for k in range(6)],
                        None if final else [field[c, x] for c in range(3)],
                        [step[c, x] for c in range(3)] if 0 < turn < 3 else None,
                    )
                )
            results = []
            for force, edges, load, block, value, before in loaded:
                gathered = [gather_rows(force[c]) for c in range(3)]
                come = pushed_along([go for stay, go in gathered], edges)
                rest = [load[c] - (gathered[c][0] + come[c]) for c in range(3)]
                if final:
                    moved = apply_inverse([entry[:ROWS] for entry in block], [part[:ROWS] for part in rest])
                    results.append((moved, None, None))
                    continue
                keep, add = weights[turn]
                moved = [add * part for part in apply_inverse(block, rest)]
                if turn > 0:
                    moved = [keep * before[c] + moved[c] for c in range(3)]
                value = [value[c] + moved[c] for c in range(3)]
                results.append((moved, value, modes_of(value, edges)))
            for x, (moved, value, onward) in zip(spots, results):
                for c in range(3):
                    if final:
                        out_residual[c, x - REACH] = moved[c]
                    else:
                        if turn < 2:
                            step[c, x] = moved[c]
                        field[c, x] = value[c]
                if not final:
                    store_modes(x, onward)

        def update_body(trip, carry, low=low, update_layers=update_layers):
            update_layers([low + TOGETHER * trip + i for i in range(TOGETHER)])
            return carry

        trips = (high - low) // TOGETHER
        lax.fori_loop(0, trips, update_body, 0)
        if final:
            done = pl.ds(0, TOGETHER * trips)
            copies.append(pltpu.make_async_copy(out_residual.at[:, done], residual_hbm.at[:, done], left.at[1]))
            copies[-1].start()
        if low + TOGETHER * trips < high:
            update_layers(list(range(low + TOGETHER * trips, high)))
        if final and TOGETHER * trips < layers:
            rest = pl.ds(TOGETHER * trips, layers - TOGETHER * trips)
            copies.append(pltpu.make_async_copy(out_residual.at[:, rest], residual_hbm.at[:, rest], left.at[2]))
            copies[-1].start()
        if turn == 2:
            for c in range(3):
                out_solution[c] = field[c, REACH : REACH + layers, :ROWS]
            copies.append(pltpu.make_async_copy(out_solution, solution_hbm, left.at[0]))
            copies[-1].start()
    for copy in copies:
        copy.wait()


def vmem(count):
    return [pl.BlockSpec(memory_space=pltpu.VMEM)] * count


def tiles(*lead):
    return jax.ShapeDtypeStruct((*lead, ROWS, LANES), F32)


def solution(mesh):
    dims = tuple(mesh.shape[axis] for axis in AXES)

    def swap(value, axis, kind):
        return lax.ppermute(value, AXES, swap_pairs(dims, axis, kind))

    def body(forcing, guess, lame, shear):
        layers = lame.shape[0]
        wide = layers + 2 * REACH
        params = pltpu.CompilerParams(vmem_limit_bytes=32 * 1024 * 1024)
        given = (forcing, guess, lame, shear)
        *fields, own, z_near, z_far = pl.pallas_call(
            pack_first,
            out_shape=[jax.ShapeDtypeStruct(a.shape, F32) for a in given] + [tiles(layers)] + [tiles(layers // 4)] * 2,
            in_specs=[pl.BlockSpec(memory_space=pltpu.HBM)] * 4,
            out_specs=vmem(7),
            scratch_shapes=[pltpu.SemaphoreType.DMA((4,))],
            compiler_params=params,
            name="pack_first",
        )(*(pltpu.with_memory_space_constraint(a, pltpu.HBM) for a in given))
        y0_near, y0_far, x_near, x_far = pl.pallas_call(
            pack_rest,
            out_shape=[tiles(4 * layers)] * 2 + [tiles(X_TILES)] * 2,
            in_specs=vmem(4),
            out_specs=vmem(4),
            compiler_params=params,
            name="pack_rest",
        )(*fields)
        z_far = swap(z_far, 2, 1)
        z_near = swap(z_near, 2, 0)
        y0_near = swap(y0_near, 1, 0)
        y0_far = swap(y0_far, 1, 1)
        full, x_near, x_far = pl.pallas_call(
            pack_second,
            out_shape=[tiles(layers), tiles(X_TILES), tiles(X_TILES)],
            in_specs=vmem(5),
            out_specs=vmem(3),
            compiler_params=params,
            name="pack_second",
        )(own, z_near, z_far, x_near, x_far)
        x_near = swap(x_near, 0, 0)
        x_far = swap(x_far, 0, 1)
        y1_near, y1_far = pl.pallas_call(
            pack_third,
            out_shape=[tiles(X_TILES + layers // 2)] * 2,
            in_specs=vmem(3),
            out_specs=vmem(2),
            compiler_params=params,
            name="pack_third",
        )(full, x_near, x_far)
        y1_near = swap(y1_near, 1, 0)
        y1_far = swap(y1_far, 1, 1)
        block = (2 * ROWS, LANES)
        return pl.pallas_call(
            smooth,
            out_shape=[tiles(3, layers), tiles(3, layers)],
            in_specs=vmem(11),
            out_specs=[pl.BlockSpec(memory_space=pltpu.HBM)] * 2,
            scratch_shapes=[
                pltpu.VMEM((3, layers, ROWS, LANES), F32),
                pltpu.VMEM((3, layers, ROWS, LANES), F32),
                pltpu.SemaphoreType.DMA((3,)),
                pltpu.VMEM((8, wide, *block), F32),
                pltpu.VMEM((wide, *block), F32),
                pltpu.VMEM((8, 3, *block), F32),
                pltpu.VMEM((6, 3, *block), F32),
                pltpu.VMEM((3, 3, *block), F32),
                pltpu.VMEM((3, 3, *block), F32),
                pltpu.VMEM((3, 3, *block), F32),
                pltpu.VMEM((6, wide, *block), F32),
                pltpu.VMEM((3, wide, *block), F32),
                pltpu.VMEM((wide, 12, *block), F32),
                pltpu.VMEM((wide, 12, *block), F32),
            ],
            compiler_params=params,
            name="smooth",
        )(*fields, full, y0_near, y0_far, x_near, x_far, y1_near, y1_far)

    in_specs = (P(None, *AXES), P(None, *AXES), P(*AXES), P(*AXES))
    out_specs = (P(None, *AXES), P(None, *AXES))
    return jax.shard_map(body, mesh=mesh, in_specs=in_specs, out_specs=out_specs, check_vma=False)
```
